128 devices in a mesh: item: 16 (over y, x_lo, core), center: 8 (over x_hi, z).
Axes of the slice: x: 4 (x_hi: 2, x_lo: 2; x = x_hi * 2 + x_lo), y: 4, z: 4, core: 2. Of those that a mesh axis runs over, the one named last changes fastest.
Arguments:
- embeddings: bfloat16 [32768, 512], P('item'), may hold values from -6 to 6
- codes: int32 [3, 32768], P(None, 'item'), may hold values from 0 to 16383, as said below
- codebooks: bfloat16 [3, 16384, 512], P(None, 'center'), may hold values from -6 to 6
Outputs:
- new_codebooks: bfloat16 [3, 16384, 512], P(None, 'center')
- final_residual: bfloat16 [32768, 512], P('item')
The draws below stay inside these ranges and needn't reach their ends.
Inputs may be any that keep to these rules, and one draw needn't show every extreme that they name: At every level, of the 2048 items of one group of consecutive items at most 32 have codes in any one aligned block of 128 consecutive centers, and in every group some block holds exactly 32.
All inputs are finite; a program needn't handle non-finite values.
Results may differ from the reference program's by a relative error of at most 0.018.
Values may be sent and summed in bfloat16 or wider, within the bound.
A program may use at most 128 MiB of HBM per device.

```python
import jax
import jax.numpy as jnp
from jax import lax

D = 512
CENTERS = 16384
LEVELS = 3
ITEM_DEV = 2048
ITEMS = 32768
SHARE = 128
CAP = 32
N_ITEM = 16
N_CENTER = 8


def draw_codes(key, part):
    key = jax.random.fold_in(key, 7)
    cells = N_CENTER * N_ITEM
    slots = cells * CAP

    def one_group(sub):
        key_a, key_b, key_c, key_d = jax.random.split(sub, 4)
        slot_cell = jnp.arange(slots, dtype=jnp.int32) // CAP
        scores = jax.random.permutation(key_a, slots).astype(jnp.int32)
        favored = jax.random.randint(key_b, (), 0, cells, dtype=jnp.int32)
        scores = jnp.where(slot_cell == favored, scores - slots, scores)
        order = jnp.argsort(scores, stable=True)
        chosen = slot_cell[order][:ITEM_DEV]
        chosen = jax.random.permutation(key_c, chosen)
        offset = jax.random.randint(key_d, (ITEM_DEV,), 0, SHARE, dtype=jnp.int32)
        return chosen * SHARE + offset
    keys = jax.random.split(key, LEVELS * N_ITEM)
    return jax.vmap(one_group)(keys).reshape(LEVELS, ITEMS).astype(jnp.int32)


def block_scale(stream_key, extent, cuts, low, largest):
    def one(position, shards_of):
        draws = jax.random.uniform(jax.random.fold_in(jax.random.fold_in(stream_key, 6), position), (shards_of,), jnp.float32, low / len(cuts), largest / len(cuts))
        return jnp.repeat(jnp.exp(draws), extent[position] // shards_of).reshape((-1,) + (1,) * (len(extent) - position - 1))

    gain = one(*cuts[0])
    for cut in cuts[1:]:
        gain = gain * one(*cut)
    return gain


def bell_draw(stream_key, shape, width, reach, cuts=(), kind=jnp.bfloat16):
    array = width * jax.random.normal(stream_key, shape, jnp.float32)
    if cuts:
        array = array * block_scale(stream_key, shape, cuts, -0.22, 0.18)
    return jnp.clip(array, -reach, reach).astype(kind)


def setup_inputs(seed: int = 0) -> dict:
    key_list = jax.random.split(jax.random.key(seed), 4)
    embeddings = bell_draw(key_list[0], (ITEMS, D), 1.0, 6.0, ((0, 16),))
    codes = draw_codes(jax.random.fold_in(key_list[3], 71), 0)
    codebooks = bell_draw(key_list[2], (LEVELS, CENTERS, D), 1.0, 6.0, ((1, 8),))
    return dict(embeddings=embeddings, codes=codes, codebooks=codebooks)


prior_weight = 1.0


def round_keep(value):
    return lax.optimization_barrier(value.astype(jnp.bfloat16)).astype(jnp.float32)


def reference(embeddings, codes, codebooks):
    residual = embeddings
    new_books = []
    for level_index in range(LEVELS):
        group_rows = residual.reshape(N_ITEM, ITEM_DEV, D)
        group_codes = codes[level_index].reshape(N_ITEM, ITEM_DEV)

        def pool_group(carry, pieces):
            rows_here, codes_here = pieces
            pooled = jax.ops.segment_sum(rows_here.astype(jnp.float32), codes_here, num_segments=CENTERS)
            tally = jax.ops.segment_sum(jnp.ones(codes_here.shape, jnp.float32), codes_here, num_segments=CENTERS)
            return (carry[0] + round_keep(pooled), carry[1] + round_keep(tally)), None

        start = (jnp.zeros((CENTERS, D), jnp.float32), jnp.zeros((CENTERS,), jnp.float32))
        (summed, number), _ = lax.scan(pool_group, start, (group_rows, group_codes))
        previous = codebooks[level_index].astype(jnp.float32)
        updated = ((summed + prior_weight * previous) / (number[:, None] + prior_weight)).astype(jnp.bfloat16)
        new_books.append(updated)
        assigned = updated[codes[level_index]].astype(jnp.float32)
        residual = (residual.astype(jnp.float32) - assigned).astype(jnp.bfloat16)
    return jnp.stack(new_books), residual
```

```python
import functools

import jax
import jax.numpy as jnp
from jax import lax
from jax.experimental import pallas as pl
from jax.experimental.pallas import tpu as pltpu
from jax.sharding import PartitionSpec as P

MESH = pl.DeviceIdType.MESH
LEVELS, ITEMS, DIM = 3, 2048, 512
N_ITEM, N_CENTER, SHARE, CAP = 16, 8, 128, 32
SLOTS = N_ITEM * CAP
HOP1, HOP2, HOME = 64, 80, ITEMS // N_CENTER
LANES = 128
F32, BF16, I32 = jnp.float32, jnp.bfloat16, jnp.int32


def iota(shape, axis):
    return lax.broadcasted_iota(I32, shape, axis)


def onehot(match):
    return match.astype(F32).astype(BF16)


def dot(a, b):
    return jnp.dot(a, b, preferred_element_type=F32)


ROW_SLOT0 = 0
ROW_OFF = 16
ROW_D1 = 28
ROW_D2 = 40
ROW_D3 = 52
ROW_POS = 64
ROWS = 80


def prep_kernel(codes_ref, out_ref):
    me = lax.axis_index("center")
    a, b = iota((LANES, 2 * LANES), 0), iota((LANES, 2 * LANES), 1)
    before = onehot((b >= LANES) | (a < b))

    def ordered(cls, n_cls, lower=None):
        member = onehot(iota((n_cls, ITEMS), 0) == cls)
        seen = jnp.zeros((n_cls, LANES), F32)
        ranks = []
        for k in range(ITEMS // LANES):
            part = member[:, k * LANES : (k + 1) * LANES]
            both = dot(part, before)
            ranks.append(jnp.sum(part.astype(F32) * (both[:, :LANES] + seen), axis=0, keepdims=True))
            seen = seen + both[:, LANES:]
        rank = jnp.concatenate(ranks, axis=1).astype(I32)
        if lower is None:
            return rank, None
        r, s = iota((n_cls, n_cls), 0), iota((n_cls, n_cls), 1)
        start = jnp.dot(lower(r, s).astype(F32), seen, precision=lax.Precision.HIGHEST, preferred_element_type=F32)
        start = jnp.concatenate([start] * (ITEMS // LANES), axis=1)
        return rank, jnp.sum(member.astype(F32) * start, axis=0, keepdims=True).astype(I32)

    def extract(pos, n_pos, attrs):
        n_hi = n_pos // LANES
        low = onehot(iota((LANES, ITEMS), 0) == jnp.where(pos >= 0, pos % LANES, -1))
        high = iota((8, ITEMS), 0) == jnp.where(pos >= 0, pos // LANES, -1)
        rows = jnp.concatenate([jnp.where(high, at, 0) for at in attrs], axis=0).astype(F32).astype(BF16)
        got = lax.dot_general(rows, low, (((1,), (1,)), ((), ())), preferred_element_type=F32).astype(I32)
        return [got[8 * k : 8 * k + n_hi] for k in range(len(attrs))]

    out_ref[...] = jnp.zeros_like(out_ref)
    shard, off, local = [], [], []
    for lev in range(LEVELS):
        code = codes_ref[lev : lev + 1, :]
        block = code // SHARE
        rank, _ = ordered(block, N_ITEM * N_CENTER)
        slot = (block % N_ITEM) * CAP + rank
        shard.append(code // (SHARE * N_ITEM))
        off.append(code % SHARE)
        local.append(jnp.where(shard[lev] == me, slot, -1))
    for k in range(ITEMS // LANES):
        out_ref[ROW_SLOT0 + k : ROW_SLOT0 + k + 1, :] = local[0][:, k * LANES : (k + 1) * LANES]

    for lev in range(LEVELS):
        here = shard[lev]
        if lev < LEVELS - 1:
            there = shard[lev + 1]
            rank, start = ordered(
                here * N_CENTER + there, N_CENTER * N_CENTER, lambda r, s: (r // N_CENTER == s // N_CENTER) & (s < r)
            )
            order = rank + start
            via, place = order % N_CENTER, order // N_CENTER
            second, _ = ordered(via * N_CENTER + there, N_CENTER * N_CENTER)
            target = [there + 1, second]
            base = HOP2
            pos3 = jnp.where(there == me, via * HOP2 + second, -1)
            slot_next = local[lev + 1]
            hi3, lo3 = extract(pos3, N_CENTER * HOP2, [jnp.maximum(slot_next, 0) // 256 + 1, jnp.maximum(slot_next, 0) % 256])
            d3 = (hi3 - 1) * 256 + lo3
            out_ref[ROW_D3 + 6 * lev : ROW_D3 + 6 * lev + 5, :] = d3
        else:
            rank, start = ordered(here, N_CENTER, lambda r, s: s < r)
            order = rank + start
            via, place = order % N_CENTER, rank // N_CENTER
            target = [jnp.ones_like(order), order // N_CENTER]
            base = HOME
            for k in range(ITEMS // LANES):
                out_ref[ROW_POS + k : ROW_POS + k + 1, :] = (via * HOME + order // N_CENTER)[:, k * LANES : (k + 1) * LANES]
        off_s, via_s, place_s = extract(local[lev], SLOTS, [off[lev] + 1, via + 1, place])
        out_ref[ROW_OFF + 4 * lev : ROW_OFF + 4 * lev + 4, :] = off_s
        out_ref[ROW_D1 + 4 * lev : ROW_D1 + 4 * lev + 4, :] = (via_s - 1) * HOP1 + place_s
        pos2 = jnp.where(via == me, here * HOP1 + place, -1)
        hi2, lo2 = extract(pos2, N_CENTER * HOP1, target)
        out_ref[ROW_D2 + 4 * lev : ROW_D2 + 4 * lev + 4, :] = (hi2 - 1) * base + lo2


ITEM_OFFSETS = [(y, x, c) for y in range(4) for x in range(2) for c in range(2)][1:]
CHIP_OFFSETS = [o for o in ITEM_OFFSETS if o[2] == 0]
CENTER_OFFSETS = [(h, z) for h in range(2) for z in range(4)][1:]


def main_kernel(
    idx_ref, emb_ref, cb_ref, books_ref, final_ref,
    cb, meta_s, meta_r, dsend, drecv, book, nres, h1s, h1r, h2s, h2r, fsend, frecv, scatter, poscol,
    cb_sem, meta_ss, meta_rs, d_ss, d_rs, g_ss, g_rs, p_ss, p_rs, h1_ss, h1_rs, h2_ss, h2_rs, f_ss, f_rs, out_sem,
):
    item, center = lax.axis_index("item"), lax.axis_index("center")
    my_y, my_x, my_c = item // 4, (item // 2) % 2, item % 2
    my_h, my_z = center // 4, center % 4

    def item_at(o):
        return ((my_y + o[0]) % 4) * 4 + ((my_x + o[1]) % 2) * 2 + (my_c + o[2]) % 2

    def item_from(o):
        return ((my_y + 4 - o[0]) % 4) * 4 + ((my_x + o[1]) % 2) * 2 + (my_c + o[2]) % 2

    def center_at(o):
        return ((my_h + o[0]) % 2) * 4 + (my_z + o[1]) % 4

    def rows(start, size, step):
        return pl.ds(pl.multiple_of(start * step, step), size)

    barrier = pltpu.get_barrier_semaphore()
    for o in ITEM_OFFSETS:
        pl.semaphore_signal(barrier, inc=1, device_id=(item_at(o), center), device_id_type=MESH)
    for o in CENTER_OFFSETS:
        pl.semaphore_signal(barrier, inc=1, device_id=(item, center_at(o)), device_id_type=MESH)

    own_cb = pltpu.make_async_copy(cb_ref.at[:, rows(item, SHARE, SHARE), :], cb, cb_sem)
    own_cb.start()

    sends = []

    def send(src, dst, ss, rs, to):
        cp = pltpu.make_async_remote_copy(
            src_ref=src, dst_ref=dst, send_sem=ss, recv_sem=rs, device_id=to, device_id_type=MESH
        )
        cp.start()
        sends.append(cp)
        return cp

    meta_s[...] = jnp.zeros_like(meta_s)
    for h in range(4):
        for lev in range(LEVELS):
            meta_s[h, lev : lev + 1, :] = idx_ref[ROW_OFF + 4 * lev + h : ROW_OFF + 4 * lev + h + 1, :]

    for k in range(ITEMS // LANES):
        row = idx_ref[ROW_SLOT0 + k : ROW_SLOT0 + k + 1, :]
        scatter[0:SLOTS, k * LANES : (k + 1) * LANES] = onehot(iota((SLOTS, LANES), 0) == row)
    dsend[0] = dot(scatter[0:SLOTS, :], emb_ref[...]).astype(BF16)

    pl.semaphore_wait(barrier, len(ITEM_OFFSETS) + len(CENTER_OFFSETS))

    metas = []
    for n, o in enumerate(ITEM_OFFSETS):
        to = item_at(o)
        metas.append(
            send(meta_s.at[to // 4], meta_r.at[item], meta_ss.at[n], meta_rs.at[n], (to, center))
        )
    meta_r[item] = meta_s[item // 4]

    def permute(first, n_in, n_out, source, out_dtype=BF16):
        parts = [
            onehot(iota((n_out, LANES), 0) == idx_ref[first + k : first + k + 1, :]) for k in range(n_in // LANES)
        ]
        return dot(jnp.concatenate(parts, axis=1), source).astype(out_dtype)

    own_rows = rows(item, CAP, CAP)
    own_block = rows(item, SHARE, SHARE)
    metas_done = False
    for lev in range(LEVELS):
        cps = []
        for n, o in enumerate(ITEM_OFFSETS):
            to = item_at(o)
            cps.append(
                send(dsend.at[lev, rows(to, CAP, CAP)], drecv.at[lev, own_rows], d_ss.at[lev, n], d_rs.at[lev, n], (to, center))
            )
        drecv[lev, own_rows, :] = dsend[lev, own_rows, :]
        if not metas_done:
            for cp in metas:
                cp.wait_recv()
            own_cb.wait()
            metas_done = True
        members = []
        lane = iota((8, LANES), 1)
        mine = (lane >= (item % 4) * CAP) & (lane < (item % 4 + 1) * CAP)
        for q in range(4):
            total = jnp.zeros((8, LANES), I32)
            for j in range(4):
                piece = jnp.where(mine, meta_r[4 * q + j], 0)
                total = total + pltpu.roll(piece, ((j + 4 - item % 4) % 4) * CAP, 1)
            members.append((iota((SHARE, LANES), 0) + 1 == total[lev : lev + 1, :]).astype(F32))
        member = jnp.concatenate(members, axis=1)
        count = jnp.sum(member, axis=1, keepdims=True)
        for cp in cps:
            cp.wait_recv()
        pooled = dot(member.astype(BF16), drecv[lev])
        updated = ((pooled + cb[lev].astype(F32)) / (count + 1.0)).astype(BF16)
        book[lev, own_block, :] = updated
        cps = []
        for n, o in enumerate(CHIP_OFFSETS):
            to = item_at(o)
            cps.append(
                send(book.at[lev, own_block], book.at[lev, own_block], g_ss.at[lev, n], g_rs.at[lev, n], (to, center))
            )
        partner = (item_at((0, 0, 1)), center)
        forwards = [send(book.at[lev, own_block], book.at[lev, own_block], p_ss.at[lev, 7], p_rs.at[lev, 7], partner)]
        assigns = []
        for h in range(4):
            row = idx_ref[ROW_OFF + 4 * lev + h : ROW_OFF + 4 * lev + h + 1, :]
            assigns.append((iota((SHARE, LANES), 0) + 1 == row).astype(F32).T.astype(BF16))
        for n, o in enumerate(CHIP_OFFSETS):
            cps[n].wait_recv()
            theirs = rows(item_from(o), SHARE, SHARE)
            forwards.append(send(book.at[lev, theirs], book.at[lev, theirs], p_ss.at[lev, n], p_rs.at[lev, n], partner))
        for cp in forwards:
            cp.wait_recv()
        out = pltpu.make_async_copy(book.at[lev], books_ref.at[lev], out_sem.at[lev])
        out.start()
        for b in range(N_ITEM):
            assigned = dot(assigns[b // 4][(b % 4) * CAP : (b % 4 + 1) * CAP, :], book[lev, b * SHARE : (b + 1) * SHARE, :])
            slots = slice(b * CAP, (b + 1) * CAP)
            nres[slots, :] = (dsend[lev, slots, :].astype(F32) - assigned.astype(BF16).astype(F32)).astype(BF16)
        h1s[lev] = permute(ROW_D1 + 4 * lev, SLOTS, N_CENTER * HOP1, nres[...])
        own = rows(center, HOP1, HOP1)
        cps = []
        for n, o in enumerate(CENTER_OFFSETS):
            to = center_at(o)
            cps.append(send(h1s.at[lev, rows(to, HOP1, HOP1)], h1r.at[lev, own], h1_ss.at[lev, n], h1_rs.at[lev, n], (item, to)))
        h1r[lev, own, :] = h1s[lev, own, :]
        for cp in cps:
            cp.wait_recv()
        if lev < LEVELS - 1:
            h2s[lev] = permute(ROW_D2 + 4 * lev, N_CENTER * HOP1, N_CENTER * HOP2, h1r[lev])
            own = rows(center, HOP2, HOP2)
            cps = []
            for n, o in enumerate(CENTER_OFFSETS):
                to = center_at(o)
                cps.append(send(h2s.at[lev, rows(to, HOP2, HOP2)], h2r.at[lev, own], h2_ss.at[lev, n], h2_rs.at[lev, n], (item, to)))
            h2r[lev, own, :] = h2s[lev, own, :]
            for cp in cps:
                cp.wait_recv()
            dsend[lev + 1] = permute(ROW_D3 + 6 * lev, N_CENTER * HOP2, SLOTS, h2r[lev])
        else:
            own = rows(center, HOME, HOME)
            frecv[own, :] = permute(ROW_D2 + 4 * lev, N_CENTER * HOP1, HOME, h1r[lev])
            cps = []
            for n, o in enumerate(CENTER_OFFSETS):
                cps.append(send(frecv.at[own], frecv.at[own], f_ss.at[n], f_rs.at[n], (item, center_at(o))))
            for k in range(ITEMS // LANES):
                row = jnp.broadcast_to(idx_ref[ROW_POS + k : ROW_POS + k + 1, :].astype(F32), (LANES, LANES))
                col = row.T.astype(I32)
                for g in range(ITEMS // LANES):
                    scatter[k * LANES : (k + 1) * LANES, g * LANES : (g + 1) * LANES] = onehot(iota((LANES, LANES), 1) + g * LANES == col)
            for cp in cps:
                cp.wait_recv()
            for k in range(ITEMS // 256):
                final_ref[k * 256 : (k + 1) * 256, :] = dot(scatter[k * 256 : (k + 1) * 256, :], frecv[...]).astype(BF16)
    for lev in range(LEVELS):
        pltpu.make_async_copy(book.at[lev], books_ref.at[lev], out_sem.at[lev]).wait()
    for cp in sends:
        cp.wait_send()


def per_device(embeddings, codes, codebooks):
    vmem = pl.BlockSpec(memory_space=pltpu.VMEM)
    hbm = pl.BlockSpec(memory_space=pl.ANY)
    idx = pl.pallas_call(
        prep_kernel,
        out_shape=jax.ShapeDtypeStruct((ROWS, LANES), I32),
        in_specs=[vmem],
        out_specs=vmem,
        compiler_params=pltpu.CompilerParams(vmem_limit_bytes=48 << 20),
    )(codes)
    dma = pltpu.SemaphoreType.DMA
    return pl.pallas_call(
        main_kernel,
        out_shape=(
            jax.ShapeDtypeStruct(codebooks.shape, BF16),
            jax.ShapeDtypeStruct(embeddings.shape, BF16),
        ),
        in_specs=[vmem, vmem, hbm],
        out_specs=(hbm, vmem),
        scratch_shapes=[
            pltpu.VMEM((LEVELS, SHARE, DIM), BF16),
            pltpu.VMEM((4, 8, LANES), I32),
            pltpu.VMEM((N_ITEM, 8, LANES), I32),
            pltpu.VMEM((LEVELS, SLOTS, DIM), BF16),
            pltpu.VMEM((LEVELS, SLOTS, DIM), BF16),
            pltpu.VMEM((LEVELS, N_ITEM * SHARE, DIM), BF16),
            pltpu.VMEM((SLOTS, DIM), BF16),
            pltpu.VMEM((LEVELS, N_CENTER * HOP1, DIM), BF16),
            pltpu.VMEM((LEVELS, N_CENTER * HOP1, DIM), BF16),
            pltpu.VMEM((LEVELS - 1, N_CENTER * HOP2, DIM), BF16),
            pltpu.VMEM((LEVELS - 1, N_CENTER * HOP2, DIM), BF16),
            pltpu.VMEM((8, LANES), F32),
            pltpu.VMEM((ITEMS, DIM), BF16),
            pltpu.VMEM((ITEMS, ITEMS), BF16),
            pltpu.VMEM((8, LANES), F32),
            dma,
            dma((15,)), dma((15,)),
            dma((LEVELS, 15)), dma((LEVELS, 15)),
            dma((LEVELS, 7)), dma((LEVELS, 7)),
            dma((LEVELS, 8)), dma((LEVELS, 8)),
            dma((LEVELS, 7)), dma((LEVELS, 7)),
            dma((LEVELS, 7)), dma((LEVELS, 7)),
            dma((7,)), dma((7,)),
            dma((LEVELS,)),
        ],
        compiler_params=pltpu.CompilerParams(collective_id=0, has_side_effects=True, vmem_limit_bytes=56 << 20),
    )(idx, embeddings, codebooks)


def solution(mesh):
    placed = (P("item", None), P(None, "item"), P(None, "center", None))
    return jax.shard_map(
        per_device,
        mesh=mesh,
        in_specs=placed,
        out_specs=(P(None, "center", None), P("item", None)),
        check_vma=False,
    )
```

```python
import functools

import jax
import jax.numpy as jnp
from jax import lax
from jax.experimental import pallas as pl
from jax.experimental.pallas import tpu as pltpu
from jax.sharding import PartitionSpec as P

MESH = pl.DeviceIdType.MESH
LEVELS, ITEMS, DIM = 3, 2048, 512
N_ITEM, N_CENTER, SHARE, CAP = 16, 8, 128, 32
SLOTS = N_ITEM * CAP
HOP1, HOP2, HOME = 64, 80, ITEMS // N_CENTER
LANES = 128
F32, BF16, I32 = jnp.float32, jnp.bfloat16, jnp.int32


def iota(shape, axis):
    return lax.broadcasted_iota(I32, shape, axis)


def onehot(match):
    return match.astype(F32).astype(BF16)


def dot(a, b):
    return jnp.dot(a, b, preferred_element_type=F32)


ROW_SLOT0 = 0
ROW_OFF = 16
ROW_D1 = 28
ROW_D2 = 40
ROW_D3 = 52
ROW_POS = 64
ROWS = 80


def prep_kernel(codes_ref, out_ref):
    me = lax.axis_index("center")
    a, b = iota((LANES, 2 * LANES), 0), iota((LANES, 2 * LANES), 1)
    before = onehot((b >= LANES) | (a < b))

    def ordered(cls, n_cls, lower=None):
        member = onehot(iota((n_cls, ITEMS), 0) == cls)
        seen = jnp.zeros((n_cls, LANES), F32)
        ranks = []
        for k in range(ITEMS // LANES):
            part = member[:, k * LANES : (k + 1) * LANES]
            both = dot(part, before)
            ranks.append(jnp.sum(part.astype(F32) * (both[:, :LANES] + seen), axis=0, keepdims=True))
            seen = seen + both[:, LANES:]
        rank = jnp.concatenate(ranks, axis=1).astype(I32)
        if lower is None:
            return rank, None
        r, s = iota((n_cls, n_cls), 0), iota((n_cls, n_cls), 1)
        start = jnp.dot(lower(r, s).astype(F32), seen, precision=lax.Precision.HIGHEST, preferred_element_type=F32)
        start = jnp.concatenate([start] * (ITEMS // LANES), axis=1)
        return rank, jnp.sum(member.astype(F32) * start, axis=0, keepdims=True).astype(I32)

    def extract(pos, n_pos, attrs):
        n_hi = n_pos // LANES
        low = onehot(iota((LANES, ITEMS), 0) == jnp.where(pos >= 0, pos % LANES, -1))
        high = iota((8, ITEMS), 0) == jnp.where(pos >= 0, pos // LANES, -1)
        rows = jnp.concatenate([jnp.where(high, at, 0) for at in attrs], axis=0).astype(F32).astype(BF16)
        got = lax.dot_general(rows, low, (((1,), (1,)), ((), ())), preferred_element_type=F32).astype(I32)
        return [got[8 * k : 8 * k + n_hi] for k in range(len(attrs))]

    out_ref[...] = jnp.zeros_like(out_ref)
    shard, off, local = [], [], []
    for lev in range(LEVELS):
        code = codes_ref[lev : lev + 1, :]
        block = code // SHARE
        rank, _ = ordered(block, N_ITEM * N_CENTER)
        slot = (block % N_ITEM) * CAP + rank
        shard.append(code // (SHARE * N_ITEM))
        off.append(code % SHARE)
        local.append(jnp.where(shard[lev] == me, slot, -1))
    for k in range(ITEMS // LANES):
        out_ref[ROW_SLOT0 + k : ROW_SLOT0 + k + 1, :] = local[0][:, k * LANES : (k + 1) * LANES]

    for lev in range(LEVELS):
        here = shard[lev]
        if lev < LEVELS - 1:
            there = shard[lev + 1]
            rank, start = ordered(
                here * N_CENTER + there, N_CENTER * N_CENTER, lambda r, s: (r // N_CENTER == s // N_CENTER) & (s < r)
            )
            order = rank + start
            via, place = order % N_CENTER, order // N_CENTER
            second, _ = ordered(via * N_CENTER + there, N_CENTER * N_CENTER)
            target = [there + 1, second]
            base = HOP2
            pos3 = jnp.where(there == me, via * HOP2 + second, -1)
            slot_next = local[lev + 1]
            hi3, lo3 = extract(pos3, N_CENTER * HOP2, [jnp.maximum(slot_next, 0) // 256 + 1, jnp.maximum(slot_next, 0) % 256])
            d3 = (hi3 - 1) * 256 + lo3
            out_ref[ROW_D3 + 6 * lev : ROW_D3 + 6 * lev + 5, :] = d3
        else:
            rank, start = ordered(here, N_CENTER, lambda r, s: s < r)
            order = rank + start
            via, place = order % N_CENTER, rank // N_CENTER
            target = [jnp.ones_like(order), order // N_CENTER]
            base = HOME
            for k in range(ITEMS // LANES):
                out_ref[ROW_POS + k : ROW_POS + k + 1, :] = (via * HOME + order // N_CENTER)[:, k * LANES : (k + 1) * LANES]
        off_s, via_s, place_s = extract(local[lev], SLOTS, [off[lev] + 1, via + 1, place])
        out_ref[ROW_OFF + 4 * lev : ROW_OFF + 4 * lev + 4, :] = off_s
        out_ref[ROW_D1 + 4 * lev : ROW_D1 + 4 * lev + 4, :] = (via_s - 1) * HOP1 + place_s
        pos2 = jnp.where(via == me, here * HOP1 + place, -1)
        hi2, lo2 = extract(pos2, N_CENTER * HOP1, target)
        out_ref[ROW_D2 + 4 * lev : ROW_D2 + 4 * lev + 4, :] = (hi2 - 1) * base + lo2


CHUNKS = 2
WIDTH = DIM // CHUNKS
ITEM_OFFSETS = [(y, x, c) for y in range(4) for x in range(2) for c in range(2)][1:]
CENTER_OFFSETS = [(h, z) for h in range(2) for z in range(4)][1:]


def main_kernel(
    idx_ref, emb_ref, cb_ref, books_ref, final_ref,
    cb, meta_s, meta_r, dsend, drecv, book, nres, h1s, h1r, h2s, h2r, frecv, scatter, member, assign, sel1, sel2, sel3,
    cb_sem, meta_ss, meta_rs, d_ss, d_rs, g_ss, g_rs, p_rs, h1_ss, h1_rs, h2_ss, h2_rs, f_ss, f_rs, out_sem,
):
    item, center = lax.axis_index("item"), lax.axis_index("center")
    my_y, my_x, my_c = item // 4, (item // 2) % 2, item % 2
    my_h, my_z = center // 4, center % 4

    def item_at(y, x, c):
        return ((my_y + y) % 4) * 4 + ((my_x + x) % 2) * 2 + (my_c + c) % 2

    def center_at(h, z):
        return ((my_h + h) % 2) * 4 + (my_z + z) % 4

    def rows(start, size, step):
        return pl.ds(pl.multiple_of(start * step, step), size)

    barrier = pltpu.get_barrier_semaphore()
    for o in ITEM_OFFSETS:
        pl.semaphore_signal(barrier, inc=1, device_id=(item_at(*o), center), device_id_type=MESH)
    for o in CENTER_OFFSETS:
        pl.semaphore_signal(barrier, inc=1, device_id=(item, center_at(*o)), device_id_type=MESH)

    own_cb = pltpu.make_async_copy(cb_ref.at[:, rows(item, SHARE, SHARE), :], cb, cb_sem)
    own_cb.start()

    def remote(src, dst, ss, rs, to):
        return pltpu.make_async_remote_copy(
            src_ref=src, dst_ref=dst, send_sem=ss, recv_sem=rs, device_id=to, device_id_type=MESH
        )

    def send(src, dst, ss, rs, to):
        cp = remote(src, dst, ss, rs, to)
        cp.start()
        return cp

    def whole(ref, ss, rs):
        return remote(ref, ref, ss, rs, (item, center))

    pending = []

    meta_s[...] = jnp.zeros_like(meta_s)
    for h in range(4):
        for lev in range(LEVELS):
            meta_s[h, lev : lev + 1, :] = idx_ref[ROW_OFF + 4 * lev + h : ROW_OFF + 4 * lev + h + 1, :]

    for k in range(ITEMS // LANES):
        row = idx_ref[ROW_SLOT0 + k : ROW_SLOT0 + k + 1, :]
        scatter[0:SLOTS, k * LANES : (k + 1) * LANES] = onehot(iota((SLOTS, LANES), 0) == row)

    def selection(ref, first, n_in, n_out):
        for k in range(n_in // LANES):
            ref[0:n_out, k * LANES : (k + 1) * LANES] = onehot(
                iota((n_out, LANES), 0) == idx_ref[first + k : first + k + 1, :]
            )

    def select(ref, n_in, n_out, source):
        return dot(ref[0:n_out, 0:n_in], source).astype(BF16)

    def receive_metas():
        whole(meta_r.at[pl.ds(0, 15)], meta_ss, meta_rs).wait_recv()
        own_cb.wait()
        lane = iota((8, LANES), 1)
        mine = (lane >= (item % 4) * CAP) & (lane < (item % 4 + 1) * CAP)
        for q in range(4):
            total = jnp.zeros((8, LANES), I32)
            for j in range(4):
                piece = jnp.where(mine, meta_r[4 * q + j], 0)
                total = total + pltpu.roll(piece, ((j + 4 - item % 4) % 4) * CAP, 1)
            for lev in range(LEVELS):
                member[lev, :, q * LANES : (q + 1) * LANES] = onehot(
                    iota((SHARE, LANES), 0) + 1 == total[lev : lev + 1, :]
                )

    def build_selections(lev):
        selection(sel1.at[lev], ROW_D1 + 4 * lev, SLOTS, N_CENTER * HOP1)
        selection(sel2.at[lev], ROW_D2 + 4 * lev, N_CENTER * HOP1, N_CENTER * HOP2 if lev < LEVELS - 1 else HOME)
        if lev < LEVELS - 1:
            selection(sel3.at[lev], ROW_D3 + 6 * lev, N_CENTER * HOP2, SLOTS)
        for h in range(4):
            row = idx_ref[ROW_OFF + 4 * lev + h : ROW_OFF + 4 * lev + h + 1, :]
            assign[lev, h * LANES : (h + 1) * LANES, :] = (
                (iota((SHARE, LANES), 0) + 1 == row).astype(F32).T.astype(BF16)
            )

    def build_scatter():
        for k in range(ITEMS // LANES):
            row = jnp.broadcast_to(idx_ref[ROW_POS + k : ROW_POS + k + 1, :].astype(F32), (LANES, LANES))
            col = row.T.astype(I32)
            for g in range(ITEMS // LANES):
                scatter[k * LANES : (k + 1) * LANES, g * LANES : (g + 1) * LANES] = onehot(
                    iota((LANES, LANES), 1) + g * LANES == col
                )

    def gather(buf, size, ring, ss, rs, got):
        half = size // 2

        def block(r, p, part=None):
            if part is None:
                return buf.at[rows(ring(r, p)[0], size, size)]
            return buf.at[rows(ring(r, p)[0] * 2 + part, half, half)]

        def move(n, at, to, part=None):
            return send(block(*at, part), block(*at, part), ss, rs.at[n], ring(*to)[1])

        up, down, over = (1, 0), (3, 0), (0, 1)
        own = (0, 0)
        first = [move(0, own, up), move(1, own, down), move(2, own, over)]
        got(*own)
        yield
        first[0].wait_recv()
        a = move(3, down, up, 0)
        first[1].wait_recv()
        d = move(6, up, down, 1)
        got(*down)
        got(*up)
        first[2].wait_recv()
        b = move(4, over, up)
        c = move(5, over, down)
        got(*over)
        yield
        a.wait_recv()
        e = move(7, (2, 0), over, 0)
        d.wait_recv()
        f = move(8, (2, 0), over, 1)
        got(2, 0)
        b.wait_recv()
        got(3, 1)
        c.wait_recv()
        got(1, 1)
        yield
        e.wait_recv()
        f.wait_recv()
        got(2, 1)

    def exchange(src, dst, size, ss, rs):
        own = rows(center, size, size)
        for o in CENTER_OFFSETS:
            to = center_at(*o)
            send(src.at[rows(to, size, size)], dst.at[own], ss, rs, (item, to))
        dst[own, :] = src[own, :]
        cp = whole(dst.at[pl.ds(0, 7 * size)], ss, rs)
        pending.append(cp)
        return cp

    own_rows = rows(item, CAP, CAP)
    own_block = rows(item, SHARE, SHARE)

    def program(k):
        cols = slice(k * WIDTH, (k + 1) * WIDTH)
        last = k == CHUNKS - 1
        dsend[0, k] = dot(scatter[0:SLOTS, :], emb_ref[:, cols]).astype(BF16)
        if k == 0:
            pl.semaphore_wait(barrier, len(ITEM_OFFSETS) + len(CENTER_OFFSETS))
            for o in ITEM_OFFSETS:
                to = item_at(*o)
                send(meta_s.at[to // 4], meta_r.at[item], meta_ss, meta_rs, (to, center))
            meta_r[item] = meta_s[item // 4]
            pending.append(whole(meta_r.at[pl.ds(0, 15)], meta_ss, meta_rs))
        for lev in range(LEVELS):
            mine, theirs, bk = dsend.at[lev, k], drecv.at[lev, k], book.at[lev, k]
            for o in ITEM_OFFSETS:
                to = item_at(*o)
                send(mine.at[rows(to, CAP, CAP)], theirs.at[own_rows], d_ss.at[lev, k], d_rs.at[lev, k], (to, center))
            theirs[own_rows, :] = mine[own_rows, :]
            arrived = whole(theirs.at[pl.ds(0, 15 * CAP)], d_ss.at[lev, k], d_rs.at[lev, k])
            pending.append(arrived)
            if last:
                build_selections(lev)
            yield
            if lev == 0 and k == 0:
                receive_metas()
            arrived.wait_recv()
            count = jnp.sum(member[lev].astype(F32), axis=1, keepdims=True)
            pooled = dot(member[lev], theirs[...])
            bk[own_block, :] = ((pooled + cb[lev, :, cols].astype(F32)) / (count + 1.0)).astype(BF16)
            partner = (item_at(0, 0, 1), center)
            passed = []

            def to_partner(r, p):
                at = bk.at[rows(item_at(r, p, 0), SHARE, SHARE)]
                passed.append(send(at, at, g_ss.at[lev, k], p_rs.at[lev, k, len(passed)], partner))

            yield from gather(
                bk, SHARE, lambda r, p: (item_at(r, p, 0), (item_at(r, p, 0), center)), g_ss.at[lev, k], g_rs.at[lev, k], to_partner
            )
            pending.append(whole(bk.at[pl.ds(0, 15 * SHARE)], g_ss.at[lev, k], g_rs.at[lev, k, 0]))
            yield
            for cp in passed:
                cp.wait_recv()
            pltpu.make_async_copy(bk, books_ref.at[lev, :, cols], out_sem.at[lev, k]).start()
            for b in range(N_ITEM):
                slots = slice(b * CAP, (b + 1) * CAP)
                assigned = dot(assign[lev, slots, :], bk[b * SHARE : (b + 1) * SHARE, :])
                nres[k, slots, :] = (mine[slots, :].astype(F32) - assigned).astype(BF16)
            h1s[lev, k] = select(sel1.at[lev], SLOTS, N_CENTER * HOP1, nres[k])
            hop = exchange(h1s.at[lev, k], h1r.at[lev, k], HOP1, h1_ss.at[lev, k], h1_rs.at[lev, k])
            if last and lev == LEVELS - 1:
                build_scatter()
            yield
            hop.wait_recv()
            if lev < LEVELS - 1:
                h2s[lev, k] = select(sel2.at[lev], N_CENTER * HOP1, N_CENTER * HOP2, h1r[lev, k])
                hop = exchange(h2s.at[lev, k], h2r.at[lev, k], HOP2, h2_ss.at[lev, k], h2_rs.at[lev, k])
                yield
                hop.wait_recv()
                dsend[lev + 1, k] = select(sel3.at[lev], N_CENTER * HOP2, SLOTS, h2r[lev, k])
            else:
                own = rows(center, HOME, HOME)
                frecv[k, own, :] = select(sel2.at[lev], N_CENTER * HOP1, HOME, h1r[lev, k])
                yield from gather(
                    frecv.at[k], HOME, lambda r, p: (center_at(p, r), (item, center_at(p, r))), f_ss.at[k], f_rs.at[k], lambda r, p: None
                )
                pending.append(whole(frecv.at[k, pl.ds(0, 7 * HOME)], f_ss.at[k], f_rs.at[k, 0]))
                for t in range(ITEMS // 256):
                    final_ref[t * 256 : (t + 1) * 256, cols] = dot(
                        scatter[t * 256 : (t + 1) * 256, :], frecv[k]
                    ).astype(BF16)

    running = [program(k) for k in range(CHUNKS)]
    while running:
        running = [p for p in running if next(p, 0) is None]

    for lev in range(LEVELS):
        for k in range(CHUNKS):
            cols = slice(k * WIDTH, (k + 1) * WIDTH)
            pltpu.make_async_copy(book.at[lev, k], books_ref.at[lev, :, cols], out_sem.at[lev, k]).wait()
    for cp in pending:
        cp.wait_send()


PART = 512
PARTS = (LEVELS + 1) * (ITEMS // PART)


def copy_kernel(a_ref, b_ref, oa_ref, ob_ref, hold, in_sem, out_sem):
    pairs = []
    for t in range(ITEMS // PART):
        part = pl.ds(t * PART, PART)
        pairs += [(a_ref.at[lev, part], oa_ref.at[lev, part]) for lev in range(LEVELS)] + [(b_ref.at[part], ob_ref.at[part])]
    ins = [pltpu.make_async_copy(src, hold.at[n], in_sem.at[n]) for n, (src, _) in enumerate(pairs)]
    outs = [pltpu.make_async_copy(hold.at[n], dst, out_sem.at[n]) for n, (_, dst) in enumerate(pairs)]
    for cp in ins:
        cp.start()
    for i, o in zip(ins, outs):
        i.wait()
        o.start()
    for cp in outs:
        cp.wait()


def per_device(embeddings, codes, codebooks):
    vmem = pl.BlockSpec(memory_space=pltpu.VMEM)
    hbm = pl.BlockSpec(memory_space=pl.ANY)
    idx = pl.pallas_call(
        prep_kernel,
        out_shape=jax.ShapeDtypeStruct((ROWS, LANES), I32),
        in_specs=[vmem],
        out_specs=vmem,
        compiler_params=pltpu.CompilerParams(vmem_limit_bytes=48 << 20),
    )(codes)
    dma = pltpu.SemaphoreType.DMA
    outs = (
        jax.ShapeDtypeStruct(codebooks.shape, BF16),
        jax.ShapeDtypeStruct(embeddings.shape, BF16),
    )
    by_chunk = (LEVELS, CHUNKS)
    books, final = pl.pallas_call(
        main_kernel,
        out_shape=outs,
        in_specs=[vmem, vmem, hbm],
        out_specs=(hbm, vmem),
        scratch_shapes=[
            pltpu.VMEM((LEVELS, SHARE, DIM), BF16),
            pltpu.VMEM((4, 8, LANES), I32),
            pltpu.VMEM((N_ITEM, 8, LANES), I32),
            pltpu.VMEM((*by_chunk, SLOTS, WIDTH), BF16),
            pltpu.VMEM((*by_chunk, SLOTS, WIDTH), BF16),
            pltpu.VMEM((*by_chunk, N_ITEM * SHARE, WIDTH), BF16),
            pltpu.VMEM((CHUNKS, SLOTS, WIDTH), BF16),
            pltpu.VMEM((*by_chunk, N_CENTER * HOP1, WIDTH), BF16),
            pltpu.VMEM((*by_chunk, N_CENTER * HOP1, WIDTH), BF16),
            pltpu.VMEM((LEVELS - 1, CHUNKS, N_CENTER * HOP2, WIDTH), BF16),
            pltpu.VMEM((LEVELS - 1, CHUNKS, N_CENTER * HOP2, WIDTH), BF16),
            pltpu.VMEM((CHUNKS, ITEMS, WIDTH), BF16),
            pltpu.VMEM((ITEMS, ITEMS), BF16),
            pltpu.VMEM((LEVELS, SHARE, SLOTS), BF16),
            pltpu.VMEM((LEVELS, SLOTS, SHARE), BF16),
            pltpu.VMEM((LEVELS, N_CENTER * HOP1, SLOTS), BF16),
            pltpu.VMEM((LEVELS, N_CENTER * HOP2, N_CENTER * HOP1), BF16),
            pltpu.VMEM((LEVELS - 1, SLOTS, N_CENTER * HOP2), BF16),
            dma,
            dma, dma,
            dma(by_chunk), dma(by_chunk),
            dma(by_chunk), dma((*by_chunk, 9)), dma((*by_chunk, 8)),
            dma(by_chunk), dma(by_chunk),
            dma(by_chunk), dma(by_chunk),
            dma((CHUNKS,)), dma((CHUNKS, 9)),
            dma(by_chunk),
        ],
        compiler_params=pltpu.CompilerParams(collective_id=0, has_side_effects=True, vmem_limit_bytes=60 << 20),
    )(idx, embeddings, codebooks)
    return pl.pallas_call(
        copy_kernel,
        out_shape=outs,
        in_specs=[hbm, hbm],
        out_specs=(hbm, hbm),
        scratch_shapes=[pltpu.VMEM((PARTS, PART, DIM), BF16), dma((PARTS,)), dma((PARTS,))],
        compiler_params=pltpu.CompilerParams(vmem_limit_bytes=60 << 20),
    )(books, final)


def solution(mesh):
    placed = (P("item", None), P(None, "item"), P(None, "center", None))
    return jax.shard_map(
        per_device,
        mesh=mesh,
        in_specs=placed,
        out_specs=(P(None, "center", None), P("item", None)),
        check_vma=False,
    )
```

```python
import functools

import jax
import jax.numpy as jnp
from jax import lax
from jax.experimental import pallas as pl
from jax.experimental.pallas import tpu as pltpu
from jax.sharding import PartitionSpec as P

MESH = pl.DeviceIdType.MESH
LEVELS, ITEMS, DIM = 3, 2048, 512
N_ITEM, N_CENTER, SHARE, CAP = 16, 8, 128, 32
SLOTS = N_ITEM * CAP
HOP1, HOP2, HOME = 64, 80, ITEMS // N_CENTER
LANES = 128
F32, BF16, I32 = jnp.float32, jnp.bfloat16, jnp.int32


def iota(shape, axis):
    return lax.broadcasted_iota(I32, shape, axis)


def onehot(match):
    return match.astype(F32).astype(BF16)


def dot(a, b):
    return jnp.dot(a, b, preferred_element_type=F32)


ROW_SLOT0 = 0
ROW_OFF = 16
ROW_D1 = 28
ROW_D2 = 40
ROW_D3 = 52
ROW_POS = 64
ROWS = 80


def prep_kernel(codes_ref, out_ref):
    me = lax.axis_index("center")
    a, b = iota((LANES, 2 * LANES), 0), iota((LANES, 2 * LANES), 1)
    before = onehot((b >= LANES) | (a < b))

    def ordered(cls, n_cls, lower=None):
        member = onehot(iota((n_cls, ITEMS), 0) == cls)
        seen = jnp.zeros((n_cls, LANES), F32)
        ranks = []
        for k in range(ITEMS // LANES):
            part = member[:, k * LANES : (k + 1) * LANES]
            both = dot(part, before)
            ranks.append(jnp.sum(part.astype(F32) * (both[:, :LANES] + seen), axis=0, keepdims=True))
            seen = seen + both[:, LANES:]
        rank = jnp.concatenate(ranks, axis=1).astype(I32)
        if lower is None:
            return rank, None
        r, s = iota((n_cls, n_cls), 0), iota((n_cls, n_cls), 1)
        start = jnp.dot(lower(r, s).astype(F32), seen, precision=lax.Precision.HIGHEST, preferred_element_type=F32)
        start = jnp.concatenate([start] * (ITEMS // LANES), axis=1)
        return rank, jnp.sum(member.astype(F32) * start, axis=0, keepdims=True).astype(I32)

    def extract(pos, n_pos, attrs):
        n_hi = n_pos // LANES
        low = onehot(iota((LANES, ITEMS), 0) == jnp.where(pos >= 0, pos % LANES, -1))
        high = iota((8, ITEMS), 0) == jnp.where(pos >= 0, pos // LANES, -1)
        rows = jnp.concatenate([jnp.where(high, at, 0) for at in attrs], axis=0).astype(F32).astype(BF16)
        got = lax.dot_general(rows, low, (((1,), (1,)), ((), ())), preferred_element_type=F32).astype(I32)
        return [got[8 * k : 8 * k + n_hi] for k in range(len(attrs))]

    out_ref[...] = jnp.zeros_like(out_ref)
    shard, off, local = [], [], []
    for lev in range(LEVELS):
        code = codes_ref[lev : lev + 1, :]
        block = code // SHARE
        rank, _ = ordered(block, N_ITEM * N_CENTER)
        slot = (block % N_ITEM) * CAP + rank
        shard.append(code // (SHARE * N_ITEM))
        off.append(code % SHARE)
        local.append(jnp.where(shard[lev] == me, slot, -1))
    for k in range(ITEMS // LANES):
        out_ref[ROW_SLOT0 + k : ROW_SLOT0 + k + 1, :] = local[0][:, k * LANES : (k + 1) * LANES]

    for lev in range(LEVELS):
        here = shard[lev]
        if lev < LEVELS - 1:
            there = shard[lev + 1]
            rank, start = ordered(
                here * N_CENTER + there, N_CENTER * N_CENTER, lambda r, s: (r // N_CENTER == s // N_CENTER) & (s < r)
            )
            order = rank + start
            via, place = order % N_CENTER, order // N_CENTER
            second, _ = ordered(via * N_CENTER + there, N_CENTER * N_CENTER)
            target = [there + 1, second]
            base = HOP2
            pos3 = jnp.where(there == me, via * HOP2 + second, -1)
            slot_next = local[lev + 1]
            hi3, lo3 = extract(pos3, N_CENTER * HOP2, [jnp.maximum(slot_next, 0) // 256 + 1, jnp.maximum(slot_next, 0) % 256])
            d3 = (hi3 - 1) * 256 + lo3
            out_ref[ROW_D3 + 6 * lev : ROW_D3 + 6 * lev + 5, :] = d3
        else:
            rank, start = ordered(here, N_CENTER, lambda r, s: s < r)
            order = rank + start
            via, place = order % N_CENTER, rank // N_CENTER
            target = [jnp.ones_like(order), order // N_CENTER]
            base = HOME
            for k in range(ITEMS // LANES):
                out_ref[ROW_POS + k : ROW_POS + k + 1, :] = (via * HOME + order // N_CENTER)[:, k * LANES : (k + 1) * LANES]
        off_s, via_s, place_s = extract(local[lev], SLOTS, [off[lev] + 1, via + 1, place])
        out_ref[ROW_OFF + 4 * lev : ROW_OFF + 4 * lev + 4, :] = off_s
        out_ref[ROW_D1 + 4 * lev : ROW_D1 + 4 * lev + 4, :] = (via_s - 1) * HOP1 + place_s
        pos2 = jnp.where(via == me, here * HOP1 + place, -1)
        hi2, lo2 = extract(pos2, N_CENTER * HOP1, target)
        out_ref[ROW_D2 + 4 * lev : ROW_D2 + 4 * lev + 4, :] = (hi2 - 1) * base + lo2


CHUNKS = 2
WIDTH = DIM // CHUNKS
ITEM_OFFSETS = [(y, x, c) for y in range(4) for x in range(2) for c in range(2)][1:]
CENTER_OFFSETS = [(h, z) for h in range(2) for z in range(4)][1:]


def main_kernel(
    idx_ref, emb_ref, cb_ref, books_ref, final_ref,
    cb, meta_s, meta_r, dsend, drecv, rsend, rrecv, book, h1s, h1r, h2s, h2r, frecv, scatter, member, members, total,
    sel1, sel2, sel3,
    cb_sem, meta_ss, meta_rs, d_ss, d_rs, r_ss, r_rs, g_ss, g_rs, p_rs, h1_ss, h1_rs, h2_ss, h2_rs, f_ss, f_rs, out_sem,
):
    item, center = lax.axis_index("item"), lax.axis_index("center")
    my_y, my_x, my_c = item // 4, (item // 2) % 2, item % 2
    my_h, my_z = center // 4, center % 4

    def item_at(y, x, c):
        return ((my_y + y) % 4) * 4 + ((my_x + x) % 2) * 2 + (my_c + c) % 2

    def center_at(h, z):
        return ((my_h + h) % 2) * 4 + (my_z + z) % 4

    def rows(start, size, step):
        return pl.ds(pl.multiple_of(start * step, step), size)

    barrier = pltpu.get_barrier_semaphore()
    for o in ITEM_OFFSETS:
        pl.semaphore_signal(barrier, inc=1, device_id=(item_at(*o), center), device_id_type=MESH)
    for o in CENTER_OFFSETS:
        pl.semaphore_signal(barrier, inc=1, device_id=(item, center_at(*o)), device_id_type=MESH)

    own_cb = pltpu.make_async_copy(cb_ref.at[:, rows(item, SHARE, SHARE), :], cb, cb_sem)
    own_cb.start()

    def remote(src, dst, ss, rs, to):
        return pltpu.make_async_remote_copy(
            src_ref=src, dst_ref=dst, send_sem=ss, recv_sem=rs, device_id=to, device_id_type=MESH
        )

    def send(src, dst, ss, rs, to):
        cp = remote(src, dst, ss, rs, to)
        cp.start()
        return cp

    def whole(ref, ss, rs):
        return remote(ref, ref, ss, rs, (item, center))

    pending = []

    meta_s[...] = jnp.zeros_like(meta_s)
    for h in range(4):
        for lev in range(LEVELS):
            meta_s[h, lev : lev + 1, :] = idx_ref[ROW_OFF + 4 * lev + h : ROW_OFF + 4 * lev + h + 1, :]

    for k in range(ITEMS // LANES):
        row = idx_ref[ROW_SLOT0 + k : ROW_SLOT0 + k + 1, :]
        scatter[0:SLOTS, k * LANES : (k + 1) * LANES] = onehot(iota((SLOTS, LANES), 0) == row)

    def selection(ref, first, n_in, n_out):
        for k in range(n_in // LANES):
            ref[0:n_out, k * LANES : (k + 1) * LANES] = onehot(
                iota((n_out, LANES), 0) == idx_ref[first + k : first + k + 1, :]
            )

    def select(ref, n_in, n_out, source):
        return dot(ref[0:n_out, 0:n_in], source).astype(BF16)

    def receive_metas():
        whole(meta_r.at[pl.ds(0, 15)], meta_ss, meta_rs).wait_recv()
        own_cb.wait()
        lane = iota((8, LANES), 1)
        mine = (lane >= (item % 4) * CAP) & (lane < (item % 4 + 1) * CAP)
        for q in range(4):
            codes = jnp.zeros((8, LANES), I32)
            for j in range(4):
                piece = jnp.where(mine, meta_r[4 * q + j], 0)
                codes = codes + pltpu.roll(piece, ((j + 4 - item % 4) % 4) * CAP, 1)
            for lev in range(LEVELS):
                part = (iota((SHARE, LANES), 0) + 1 == codes[lev : lev + 1, :]).astype(F32)
                member[lev, :, q * LANES : (q + 1) * LANES] = part.astype(BF16)
                members[lev, q * LANES : (q + 1) * LANES, :] = part.T.astype(BF16)
        for lev in range(LEVELS):
            count = jnp.sum(member[lev].astype(F32), axis=1, keepdims=True)
            total[lev] = jnp.broadcast_to(count + 1.0, (SHARE, LANES))

    def build_selections(lev):
        selection(sel1.at[lev], ROW_D1 + 4 * lev, SLOTS, N_CENTER * HOP1)
        selection(sel2.at[lev], ROW_D2 + 4 * lev, N_CENTER * HOP1, N_CENTER * HOP2 if lev < LEVELS - 1 else HOME)
        if lev < LEVELS - 1:
            selection(sel3.at[lev], ROW_D3 + 6 * lev, N_CENTER * HOP2, SLOTS)

    def build_scatter():
        for k in range(ITEMS // LANES):
            row = jnp.broadcast_to(idx_ref[ROW_POS + k : ROW_POS + k + 1, :].astype(F32), (LANES, LANES))
            col = row.T.astype(I32)
            for g in range(ITEMS // LANES):
                scatter[k * LANES : (k + 1) * LANES, g * LANES : (g + 1) * LANES] = onehot(
                    iota((LANES, LANES), 1) + g * LANES == col
                )

    def mover(buf, size, ring, ss, rs):
        def move(n, at, to, part=None):
            index = ring(*at)[0]
            if part is None:
                piece = buf.at[rows(index, size, size)]
            else:
                piece = buf.at[rows(index * 2 + part, size // 2, size // 2)]
            return send(piece, piece, ss, rs.at[n], ring(*to)[1])

        return move

    own, up, down, over = (0, 0), (1, 0), (3, 0), (0, 1)

    def gather_rows(k):
        move = mover(frecv.at[k], HOME, lambda z, h: (center_at(h, z), (item, center_at(h, z))), f_ss.at[k], f_rs.at[k])
        first = [move(0, own, up), move(1, own, down), move(2, own, over)]
        yield
        first[0].wait_recv()
        a = move(3, down, up, 0)
        first[1].wait_recv()
        d = move(4, up, down, 1)
        first[2].wait_recv()
        rest = [move(5, over, up), move(6, over, down)]
        yield
        a.wait_recv()
        rest.append(move(7, (2, 0), over, 0))
        d.wait_recv()
        rest.append(move(8, (2, 0), over, 1))
        yield
        for cp in rest:
            cp.wait_recv()

    def gather_books(lev, k):
        bk, cols = book.at[lev, k], slice(k * WIDTH, (k + 1) * WIDTH)
        move = mover(
            bk, SHARE,
            lambda y, x: (my_c * 8 + item_at(y, x, 0) // 2, (item_at(y, x, 0), center)),
            g_ss.at[lev, k], g_rs.at[lev, k],
        )
        first = [move(0, own, up), move(1, own, down), move(2, own, over)]
        yield
        for cp in first:
            cp.wait_recv()
        second = [move(3, down, up, 0), move(4, up, down, 1), move(5, over, up), move(6, over, down)]
        yield
        second[2].wait_recv()
        third = [move(7, (3, 1), up, 0)]
        second[3].wait_recv()
        third.append(move(8, (1, 1), down, 1))
        yield
        for cp in second[:2] + third:
            cp.wait_recv()
        half = bk.at[rows(my_c, 8 * SHARE, 8 * SHARE)]
        passed = send(half, half, g_ss.at[lev, k], p_rs.at[lev, k], (item_at(0, 0, 1), center))
        yield
        passed.wait_recv()
        for c in range(2):
            for q in range(8):
                pltpu.make_async_copy(
                    bk.at[pl.ds((c * 8 + q) * SHARE, SHARE)], books_ref.at[lev, q, c, :, cols], out_sem.at[lev, k]
                ).start()
        pending.append(whole(bk.at[pl.ds(0, 15 * SHARE)], g_ss.at[lev, k], p_rs.at[lev, k]))

    def exchange(src, dst, size, ss, rs):
        own = rows(center, size, size)
        for o in CENTER_OFFSETS:
            to = center_at(*o)
            send(src.at[rows(to, size, size)], dst.at[own], ss, rs, (item, to))
        dst[own, :] = src[own, :]
        cp = whole(dst.at[pl.ds(0, 7 * size)], ss, rs)
        pending.append(cp)
        return cp

    def swap(src, dst, ss, rs):
        own_rows = rows(item, CAP, CAP)
        for o in ITEM_OFFSETS:
            to = item_at(*o)
            send(src.at[rows(to, CAP, CAP)], dst.at[own_rows], ss, rs, (to, center))
        dst[own_rows, :] = src[own_rows, :]
        cp = whole(dst.at[pl.ds(0, 15 * CAP)], ss, rs)
        pending.append(cp)
        return cp

    def program(k):
        cols = slice(k * WIDTH, (k + 1) * WIDTH)
        last = k == CHUNKS - 1
        background = []

        def step():
            background[:] = [g for g in background if next(g, 0) is None]

        dsend[0, k] = dot(scatter[0:SLOTS, :], emb_ref[:, cols]).astype(BF16)
        if k == 0:
            pl.semaphore_wait(barrier, len(ITEM_OFFSETS) + len(CENTER_OFFSETS))
            for o in ITEM_OFFSETS:
                to = item_at(*o)
                send(meta_s.at[to // 4], meta_r.at[item], meta_ss, meta_rs, (to, center))
            meta_r[item] = meta_s[item // 4]
            pending.append(whole(meta_r.at[pl.ds(0, 15)], meta_ss, meta_rs))
        for lev in range(LEVELS):
            arrived = swap(dsend.at[lev, k], drecv.at[lev, k], d_ss.at[lev, k], d_rs.at[lev, k])
            step()
            if last:
                build_selections(lev)
            yield
            if lev == 0 and k == 0:
                receive_metas()
            arrived.wait_recv()
            pooled = dot(member[lev], drecv[lev, k])
            size = jnp.concatenate([total[lev]] * (WIDTH // LANES), axis=1)
            updated = ((pooled + cb[lev, :, cols].astype(F32)) / size).astype(BF16)
            rsend[lev, k] = (drecv[lev, k].astype(F32) - dot(members[lev], updated)).astype(BF16)
            arrived = swap(rsend.at[lev, k], rrecv.at[lev, k], r_ss.at[lev, k], r_rs.at[lev, k])
            book[lev, k, rows(my_c * 8 + item // 2, SHARE, SHARE), :] = updated
            step()
            background.append(gather_books(lev, k))
            next(background[-1])
            yield
            arrived.wait_recv()
            h1s[lev, k] = select(sel1.at[lev], SLOTS, N_CENTER * HOP1, rrecv[lev, k])
            hop = exchange(h1s.at[lev, k], h1r.at[lev, k], HOP1, h1_ss.at[lev, k], h1_rs.at[lev, k])
            step()
            if last and lev == LEVELS - 1:
                build_scatter()
            yield
            hop.wait_recv()
            if lev < LEVELS - 1:
                h2s[lev, k] = select(sel2.at[lev], N_CENTER * HOP1, N_CENTER * HOP2, h1r[lev, k])
                hop = exchange(h2s.at[lev, k], h2r.at[lev, k], HOP2, h2_ss.at[lev, k], h2_rs.at[lev, k])
                step()
                yield
                hop.wait_recv()
                dsend[lev + 1, k] = select(sel3.at[lev], N_CENTER * HOP2, SLOTS, h2r[lev, k])
            else:
                frecv[k, rows(center, HOME, HOME), :] = select(sel2.at[lev], N_CENTER * HOP1, HOME, h1r[lev, k])
                for _ in gather_rows(k):
                    step()
                    yield
                while background:
                    step()
                pending.append(whole(frecv.at[k, pl.ds(0, 7 * HOME)], f_ss.at[k], f_rs.at[k, 0]))
                for t in range(ITEMS // 256):
                    final_ref[t * 256 : (t + 1) * 256, cols] = dot(
                        scatter[t * 256 : (t + 1) * 256, :], frecv[k]
                    ).astype(BF16)

    running = [program(k) for k in range(CHUNKS)]
    while running:
        running = [p for p in running if next(p, 0) is None]

    for lev in range(LEVELS):
        for k in range(CHUNKS):
            pltpu.make_async_copy(book.at[lev, k], book.at[lev, k], out_sem.at[lev, k]).wait()
    for cp in pending:
        cp.wait_send()


PART = 512
PARTS = (LEVELS + 1) * (ITEMS // PART)


def copy_kernel(a_ref, b_ref, oa_ref, ob_ref, hold, in_sem, out_sem):
    pairs = []
    for t in range(ITEMS // PART):
        part = pl.ds(t * PART, PART)
        pairs += [(a_ref.at[lev, part], oa_ref.at[lev, part]) for lev in range(LEVELS)] + [(b_ref.at[part], ob_ref.at[part])]
    ins = [pltpu.make_async_copy(src, hold.at[n], in_sem.at[n]) for n, (src, _) in enumerate(pairs)]
    outs = [pltpu.make_async_copy(hold.at[n], dst, out_sem.at[n]) for n, (_, dst) in enumerate(pairs)]
    for cp in ins:
        cp.start()
    for i, o in zip(ins, outs):
        i.wait()
        o.start()
    for cp in outs:
        cp.wait()


def per_device(embeddings, codes, codebooks):
    vmem = pl.BlockSpec(memory_space=pltpu.VMEM)
    hbm = pl.BlockSpec(memory_space=pl.ANY)
    idx = pl.pallas_call(
        prep_kernel,
        out_shape=jax.ShapeDtypeStruct((ROWS, LANES), I32),
        in_specs=[vmem],
        out_specs=vmem,
        compiler_params=pltpu.CompilerParams(vmem_limit_bytes=48 << 20),
    )(codes)
    dma = pltpu.SemaphoreType.DMA
    outs = (
        jax.ShapeDtypeStruct(codebooks.shape, BF16),
        jax.ShapeDtypeStruct(embeddings.shape, BF16),
    )
    by_chunk = (LEVELS, CHUNKS)
    books, final = pl.pallas_call(
        main_kernel,
        out_shape=(jax.ShapeDtypeStruct((LEVELS, N_ITEM // 2, 2, SHARE, DIM), BF16), outs[1]),
        in_specs=[vmem, vmem, hbm],
        out_specs=(hbm, vmem),
        scratch_shapes=[
            pltpu.VMEM((LEVELS, SHARE, DIM), BF16),
            pltpu.VMEM((4, 8, LANES), I32),
            pltpu.VMEM((N_ITEM, 8, LANES), I32),
            pltpu.VMEM((*by_chunk, SLOTS, WIDTH), BF16),
            pltpu.VMEM((*by_chunk, SLOTS, WIDTH), BF16),
            pltpu.VMEM((*by_chunk, SLOTS, WIDTH), BF16),
            pltpu.VMEM((*by_chunk, SLOTS, WIDTH), BF16),
            pltpu.VMEM((*by_chunk, N_ITEM * SHARE, WIDTH), BF16),
            pltpu.VMEM((*by_chunk, N_CENTER * HOP1, WIDTH), BF16),
            pltpu.VMEM((*by_chunk, N_CENTER * HOP1, WIDTH), BF16),
            pltpu.VMEM((LEVELS - 1, CHUNKS, N_CENTER * HOP2, WIDTH), BF16),
            pltpu.VMEM((LEVELS - 1, CHUNKS, N_CENTER * HOP2, WIDTH), BF16),
            pltpu.VMEM((CHUNKS, ITEMS, WIDTH), BF16),
            pltpu.VMEM((ITEMS, ITEMS), BF16),
            pltpu.VMEM((LEVELS, SHARE, SLOTS), BF16),
            pltpu.VMEM((LEVELS, SLOTS, SHARE), BF16),
            pltpu.VMEM((LEVELS, SHARE, LANES), F32),
            pltpu.VMEM((LEVELS, N_CENTER * HOP1, SLOTS), BF16),
            pltpu.VMEM((LEVELS, N_CENTER * HOP2, N_CENTER * HOP1), BF16),
            pltpu.VMEM((LEVELS - 1, SLOTS, N_CENTER * HOP2), BF16),
            dma,
            dma, dma,
            dma(by_chunk), dma(by_chunk),
            dma(by_chunk), dma(by_chunk),
            dma(by_chunk), dma((*by_chunk, 9)), dma(by_chunk),
            dma(by_chunk), dma(by_chunk),
            dma(by_chunk), dma(by_chunk),
            dma((CHUNKS,)), dma((CHUNKS, 9)),
            dma(by_chunk),
        ],
        compiler_params=pltpu.CompilerParams(collective_id=0, has_side_effects=True, vmem_limit_bytes=60 << 20),
    )(idx, embeddings, codebooks)
    return pl.pallas_call(
        copy_kernel,
        out_shape=outs,
        in_specs=[hbm, hbm],
        out_specs=(hbm, hbm),
        scratch_shapes=[pltpu.VMEM((PARTS, PART, DIM), BF16), dma((PARTS,)), dma((PARTS,))],
        compiler_params=pltpu.CompilerParams(vmem_limit_bytes=60 << 20),
    )(books.reshape(codebooks.shape), final)


def solution(mesh):
    placed = (P("item", None), P(None, "item"), P(None, "center", None))
    return jax.shard_map(
        per_device,
        mesh=mesh,
        in_specs=placed,
        out_specs=(P(None, "center", None), P("item", None)),
        check_vma=False,
    )
```

```python
import functools

import jax
import jax.numpy as jnp
from jax import lax
from jax.experimental import pallas as pl
from jax.experimental.pallas import tpu as pltpu
from jax.sharding import PartitionSpec as P

MESH = pl.DeviceIdType.MESH
LEVELS, ITEMS, DIM = 3, 2048, 512
N_ITEM, N_CENTER, SHARE, CAP = 16, 8, 128, 32
SLOTS = N_ITEM * CAP
HOP1, HOP2, HOME = 64, 80, ITEMS // N_CENTER
LANES = 128
F32, BF16, I32 = jnp.float32, jnp.bfloat16, jnp.int32


def iota(shape, axis):
    return lax.broadcasted_iota(I32, shape, axis)


def onehot(match):
    return match.astype(F32).astype(BF16)


def dot(a, b):
    return jnp.dot(a, b, preferred_element_type=F32)


ROW_OFF = 0
ROW_D1 = 12
ROW_D2 = 24
ROW_D3 = 36
ROW_POS = 48
ROWS = 64


def ordered(cls, n_cls, lower=None):
    a, b = iota((LANES, 2 * LANES), 0), iota((LANES, 2 * LANES), 1)
    before = onehot((b >= LANES) | (a < b))
    member = onehot(iota((n_cls, ITEMS), 0) == cls)
    seen = jnp.zeros((n_cls, LANES), F32)
    ranks = []
    for k in range(ITEMS // LANES):
        part = member[:, k * LANES : (k + 1) * LANES]
        both = dot(part, before)
        ranks.append(jnp.sum(part.astype(F32) * (both[:, :LANES] + seen), axis=0, keepdims=True))
        seen = seen + both[:, LANES:]
    rank = jnp.concatenate(ranks, axis=1).astype(I32)
    if lower is None:
        return rank, None
    r, s = iota((n_cls, n_cls), 0), iota((n_cls, n_cls), 1)
    start = jnp.dot(lower(r, s).astype(F32), seen, precision=lax.Precision.HIGHEST, preferred_element_type=F32)
    start = jnp.concatenate([start] * (ITEMS // LANES), axis=1)
    return rank, jnp.sum(member.astype(F32) * start, axis=0, keepdims=True).astype(I32)


def extract(pos, n_pos, attrs):
    n_hi = n_pos // LANES
    low = onehot(iota((LANES, ITEMS), 0) == jnp.where(pos >= 0, pos & (LANES - 1), -1))
    high = iota((8, ITEMS), 0) == jnp.where(pos >= 0, pos >> 7, -1)
    rows = jnp.concatenate([jnp.where(high, at, 0) for at in attrs], axis=0).astype(F32).astype(BF16)
    got = lax.dot_general(rows, low, (((1,), (1,)), ((), ())), preferred_element_type=F32).astype(I32)
    return [got[8 * k : 8 * k + n_hi] for k in range(len(attrs))]


def slots_of(codes_ref, lev, me):
    code = codes_ref[lev : lev + 1, :]
    block = code >> 7
    rank, _ = ordered(block, N_ITEM * N_CENTER)
    shard = code >> 11
    return shard, code & (SHARE - 1), jnp.where(shard == me, (block & (N_ITEM - 1)) * CAP + rank, -1)


def prepare_codes(idx, lev, off, local):
    idx[ROW_OFF + 4 * lev : ROW_OFF + 4 * lev + 4, :] = extract(local, SLOTS, [off + 1])[0]


def prepare_moves(idx, lev, me, here, local, there, slot_next):
    if lev < LEVELS - 1:
        rank, start = ordered(here * N_CENTER + there, N_CENTER * N_CENTER, lambda r, s: (r // N_CENTER == s // N_CENTER) & (s < r))
        order = rank + start
        via, place = order & 7, order >> 3
        second, _ = ordered(via * N_CENTER + there, N_CENTER * N_CENTER)
        target = [there + 1, second]
        base = HOP2
        pos3 = jnp.where(there == me, via * HOP2 + second, -1)
        slot_next = jnp.maximum(slot_next, 0)
        hi3, lo3 = extract(pos3, N_CENTER * HOP2, [(slot_next >> 8) + 1, slot_next & 255])
        idx[ROW_D3 + 6 * lev : ROW_D3 + 6 * lev + 5, :] = (hi3 - 1) * 256 + lo3
    else:
        rank, start = ordered(here, N_CENTER, lambda r, s: s < r)
        order = rank + start
        via, place = order & 7, rank >> 3
        target = [jnp.ones_like(order), order >> 3]
        base = HOME
        for k in range(ITEMS // LANES):
            idx[ROW_POS + k : ROW_POS + k + 1, :] = (via * HOME + (order >> 3))[:, k * LANES : (k + 1) * LANES]
    via_s, place_s = extract(local, SLOTS, [via + 1, place])
    idx[ROW_D1 + 4 * lev : ROW_D1 + 4 * lev + 4, :] = (via_s - 1) * HOP1 + place_s
    pos2 = jnp.where(via == me, here * HOP1 + place, -1)
    hi2, lo2 = extract(pos2, N_CENTER * HOP1, target)
    idx[ROW_D2 + 4 * lev : ROW_D2 + 4 * lev + 4, :] = (hi2 - 1) * base + lo2


CHUNKS = 2
WIDTH = DIM // CHUNKS
ITEM_OFFSETS = [(y, x, c) for y in range(4) for x in range(2) for c in range(2)][1:]
CENTER_OFFSETS = [(h, z) for h in range(2) for z in range(4)][1:]


def main_kernel(
    codes_hbm, emb_hbm, cb_ref, books_ref, final_ref,
    codes_ref, emb, idx_ref, cb, meta_s, meta_r, dsend, drecv, rsend, rrecv, book, h1s, h1r, h2s, h2r, frecv, scatter, member, members, total,
    sel1, sel2, sel3,
    codes_sem, emb_sem, cb_sem, meta_ss, meta_rs, d_ss, d_rs, r_ss, r_rs, g_ss, g_rs, p_rs, h1_ss, h1_rs, h2_ss, h2_rs, f_ss, f_rs, out_sem,
):
    item, center = lax.axis_index("item"), lax.axis_index("center")
    my_y, my_x, my_c = item // 4, (item // 2) % 2, item % 2
    my_h, my_z = center // 4, center % 4

    def item_at(y, x, c):
        return ((my_y + y) % 4) * 4 + ((my_x + x) % 2) * 2 + (my_c + c) % 2

    def center_at(h, z):
        return ((my_h + h) % 2) * 4 + (my_z + z) % 4

    def rows(start, size, step):
        return pl.ds(pl.multiple_of(start * step, step), size)

    own_codes = pltpu.make_async_copy(codes_hbm, codes_ref, codes_sem)
    own_codes.start()
    own_emb = pltpu.make_async_copy(emb_hbm, emb, emb_sem)
    own_emb.start()
    barrier = pltpu.get_barrier_semaphore()
    for o in ITEM_OFFSETS:
        pl.semaphore_signal(barrier, inc=1, device_id=(item_at(*o), center), device_id_type=MESH)
    for o in CENTER_OFFSETS:
        pl.semaphore_signal(barrier, inc=1, device_id=(item, center_at(*o)), device_id_type=MESH)

    own_cb = pltpu.make_async_copy(cb_ref.at[:, rows(item, SHARE, SHARE), :], cb, cb_sem)
    own_cb.start()

    def remote(src, dst, ss, rs, to):
        return pltpu.make_async_remote_copy(
            src_ref=src, dst_ref=dst, send_sem=ss, recv_sem=rs, device_id=to, device_id_type=MESH
        )

    def send(src, dst, ss, rs, to):
        cp = remote(src, dst, ss, rs, to)
        cp.start()
        return cp

    def whole(ref, ss, rs):
        return remote(ref, ref, ss, rs, (item, center))

    pending = []

    own_codes.wait()
    known = [slots_of(codes_ref, 0, center)]
    for k in range(ITEMS // LANES):
        row = known[0][2][:, k * LANES : (k + 1) * LANES]
        scatter[0:SLOTS, k * LANES : (k + 1) * LANES] = onehot(iota((SLOTS, LANES), 0) == row)
    own_emb.wait()

    def send_metas():
        for lev in range(1, LEVELS):
            known.append(slots_of(codes_ref, lev, center))
        for lev in range(LEVELS):
            prepare_codes(idx_ref, lev, *known[lev][1:])
        meta_s[...] = jnp.zeros_like(meta_s)
        for h in range(4):
            for lev in range(LEVELS):
                meta_s[h, lev : lev + 1, :] = idx_ref[ROW_OFF + 4 * lev + h : ROW_OFF + 4 * lev + h + 1, :]
        for o in ITEM_OFFSETS:
            to = item_at(*o)
            send(meta_s.at[to // 4], meta_r.at[item], meta_ss, meta_rs, (to, center))
        meta_r[item] = meta_s[item // 4]
        pending.append(whole(meta_r.at[pl.ds(0, 15)], meta_ss, meta_rs))

    def selection(ref, first, n_in, n_out):
        for k in range(n_in // LANES):
            ref[0:n_out, k * LANES : (k + 1) * LANES] = onehot(
                iota((n_out, LANES), 0) == idx_ref[first + k : first + k + 1, :]
            )

    def select(ref, n_in, n_out, source):
        return dot(ref[0:n_out, 0:n_in], source).astype(BF16)

    def receive_metas():
        whole(meta_r.at[pl.ds(0, 15)], meta_ss, meta_rs).wait_recv()
        own_cb.wait()
        lane = iota((8, LANES), 1)
        mine = (lane >= (item % 4) * CAP) & (lane < (item % 4 + 1) * CAP)
        for q in range(4):
            codes = jnp.zeros((8, LANES), I32)
            for j in range(4):
                piece = jnp.where(mine, meta_r[4 * q + j], 0)
                codes = codes + pltpu.roll(piece, ((j + 4 - item % 4) % 4) * CAP, 1)
            for lev in range(LEVELS):
                part = (iota((SHARE, LANES), 0) + 1 == codes[lev : lev + 1, :]).astype(F32)
                member[lev, :, q * LANES : (q + 1) * LANES] = part.astype(BF16)
                members[lev, q * LANES : (q + 1) * LANES, :] = part.T.astype(BF16)
        for lev in range(LEVELS):
            count = jnp.sum(member[lev].astype(F32), axis=1, keepdims=True)
            total[lev] = jnp.broadcast_to(count + 1.0, (SHARE, LANES))

    def build_selections(lev):
        nxt = known[min(lev + 1, LEVELS - 1)]
        prepare_moves(idx_ref, lev, center, known[lev][0], known[lev][2], nxt[0], nxt[2])
        selection(sel1.at[lev], ROW_D1 + 4 * lev, SLOTS, N_CENTER * HOP1)
        selection(sel2.at[lev], ROW_D2 + 4 * lev, N_CENTER * HOP1, N_CENTER * HOP2 if lev < LEVELS - 1 else HOME)
        if lev < LEVELS - 1:
            selection(sel3.at[lev], ROW_D3 + 6 * lev, N_CENTER * HOP2, SLOTS)

    def build_scatter():
        for k in range(ITEMS // LANES):
            row = jnp.broadcast_to(idx_ref[ROW_POS + k : ROW_POS + k + 1, :].astype(F32), (LANES, LANES))
            col = row.T.astype(I32)
            for g in range(ITEMS // LANES):
                scatter[k * LANES : (k + 1) * LANES, g * LANES : (g + 1) * LANES] = onehot(
                    iota((LANES, LANES), 1) + g * LANES == col
                )

    def mover(buf, size, ring, ss, rs):
        def move(n, at, to, part=None):
            index = ring(*at)[0]
            if part is None:
                piece = buf.at[rows(index, size, size)]
            else:
                piece = buf.at[rows(index * 2 + part, size // 2, size // 2)]
            return send(piece, piece, ss, rs.at[n], ring(*to)[1])

        return move

    own, up, down, over = (0, 0), (1, 0), (3, 0), (0, 1)

    def gather_rows(k):
        move = mover(frecv.at[k], HOME, lambda z, h: (center_at(h, z), (item, center_at(h, z))), f_ss.at[k], f_rs.at[k])
        first = [move(0, own, up), move(1, own, down), move(2, own, over)]
        yield
        first[0].wait_recv()
        a = move(3, down, up, 0)
        first[1].wait_recv()
        d = move(4, up, down, 1)
        first[2].wait_recv()
        rest = [move(5, over, up), move(6, over, down)]
        yield
        a.wait_recv()
        rest.append(move(7, (2, 0), over, 0))
        d.wait_recv()
        rest.append(move(8, (2, 0), over, 1))
        yield
        for cp in rest:
            cp.wait_recv()

    def gather_books(lev, k):
        bk, cols = book.at[lev, k], slice(k * WIDTH, (k + 1) * WIDTH)
        move = mover(
            bk, SHARE,
            lambda y, x: (my_c * 8 + item_at(y, x, 0) // 2, (item_at(y, x, 0), center)),
            g_ss.at[lev, k], g_rs.at[lev, k],
        )
        first = [move(0, own, up), move(1, own, down), move(2, own, over)]
        yield
        for cp in first:
            cp.wait_recv()
        second = [move(3, down, up, 0), move(4, up, down, 1), move(5, over, up), move(6, over, down)]
        yield
        second[2].wait_recv()
        third = [move(7, (3, 1), up, 0)]
        second[3].wait_recv()
        third.append(move(8, (1, 1), down, 1))
        yield
        for cp in second[:2] + third:
            cp.wait_recv()
        half = bk.at[rows(my_c, 8 * SHARE, 8 * SHARE)]
        passed = send(half, half, g_ss.at[lev, k], p_rs.at[lev, k], (item_at(0, 0, 1), center))
        yield
        passed.wait_recv()
        for c in range(2):
            for q in range(8):
                pltpu.make_async_copy(
                    bk.at[pl.ds((c * 8 + q) * SHARE, SHARE)], books_ref.at[lev, q, c, :, cols], out_sem.at[lev, k]
                ).start()
        pending.append(whole(bk.at[pl.ds(0, 15 * SHARE)], g_ss.at[lev, k], p_rs.at[lev, k]))

    def exchange(src, dst, size, ss, rs):
        own = rows(center, size, size)
        for o in CENTER_OFFSETS:
            to = center_at(*o)
            send(src.at[rows(to, size, size)], dst.at[own], ss, rs, (item, to))
        dst[own, :] = src[own, :]
        cp = whole(dst.at[pl.ds(0, 7 * size)], ss, rs)
        pending.append(cp)
        return cp

    def swap(src, dst, ss, rs):
        own_rows = rows(item, CAP, CAP)
        for o in ITEM_OFFSETS:
            to = item_at(*o)
            send(src.at[rows(to, CAP, CAP)], dst.at[own_rows], ss, rs, (to, center))
        dst[own_rows, :] = src[own_rows, :]
        cp = whole(dst.at[pl.ds(0, 15 * CAP)], ss, rs)
        pending.append(cp)
        return cp

    def program(k):
        cols = slice(k * WIDTH, (k + 1) * WIDTH)
        last = k == CHUNKS - 1
        background = []

        def step():
            background[:] = [g for g in background if next(g, 0) is None]

        dsend[0, k] = dot(scatter[0:SLOTS, :], emb[:, cols]).astype(BF16)
        if k == 0:
            pl.semaphore_wait(barrier, len(ITEM_OFFSETS) + len(CENTER_OFFSETS))
        for lev in range(LEVELS):
            arrived = swap(dsend.at[lev, k], drecv.at[lev, k], d_ss.at[lev, k], d_rs.at[lev, k])
            step()
            if last:
                if lev == 0:
                    send_metas()
                build_selections(lev)
            yield
            if lev == 0 and k == 0:
                receive_metas()
            arrived.wait_recv()
            pooled = dot(member[lev], drecv[lev, k])
            size = jnp.concatenate([total[lev]] * (WIDTH // LANES), axis=1)
            updated = ((pooled + cb[lev, :, cols].astype(F32)) / size).astype(BF16)
            rsend[lev, k] = (drecv[lev, k].astype(F32) - dot(members[lev], updated)).astype(BF16)
            arrived = swap(rsend.at[lev, k], rrecv.at[lev, k], r_ss.at[lev, k], r_rs.at[lev, k])
            book[lev, k, rows(my_c * 8 + item // 2, SHARE, SHARE), :] = updated
            step()
            background.append(gather_books(lev, k))
            next(background[-1])
            yield
            arrived.wait_recv()
            h1s[lev, k] = select(sel1.at[lev], SLOTS, N_CENTER * HOP1, rrecv[lev, k])
            hop = exchange(h1s.at[lev, k], h1r.at[lev, k], HOP1, h1_ss.at[lev, k], h1_rs.at[lev, k])
            step()
            if last and lev == LEVELS - 1:
                build_scatter()
            yield
            hop.wait_recv()
            if lev < LEVELS - 1:
                h2s[lev, k] = select(sel2.at[lev], N_CENTER * HOP1, N_CENTER * HOP2, h1r[lev, k])
                hop = exchange(h2s.at[lev, k], h2r.at[lev, k], HOP2, h2_ss.at[lev, k], h2_rs.at[lev, k])
                step()
                yield
                hop.wait_recv()
                dsend[lev + 1, k] = select(sel3.at[lev], N_CENTER * HOP2, SLOTS, h2r[lev, k])
            else:
                frecv[k, rows(center, HOME, HOME), :] = select(sel2.at[lev], N_CENTER * HOP1, HOME, h1r[lev, k])
                for _ in gather_rows(k):
                    step()
                    yield
                while background:
                    step()
                pending.append(whole(frecv.at[k, pl.ds(0, 7 * HOME)], f_ss.at[k], f_rs.at[k, 0]))
                for t in range(ITEMS // 256):
                    final_ref[t * 256 : (t + 1) * 256, cols] = dot(
                        scatter[t * 256 : (t + 1) * 256, :], frecv[k]
                    ).astype(BF16)

    running = [program(k) for k in range(CHUNKS)]
    while running:
        running = [p for p in running if next(p, 0) is None]

    for lev in range(LEVELS):
        for k in range(CHUNKS):
            pltpu.make_async_copy(book.at[lev, k], book.at[lev, k], out_sem.at[lev, k]).wait()
    for cp in pending:
        cp.wait_send()


def copy_kernel(a_ref, b_ref, oa_ref, ob_ref, sem):
    pairs = [(b_ref, ob_ref)] + [(a_ref.at[lev], oa_ref.at[lev]) for lev in range(LEVELS)]
    cps = [pltpu.make_async_copy(src, dst, sem.at[n]) for n, (src, dst) in enumerate(pairs)]
    for cp in cps:
        cp.start()
    for cp in cps:
        cp.wait()


def per_device(embeddings, codes, codebooks):
    vmem = pl.BlockSpec(memory_space=pltpu.VMEM)
    hbm = pl.BlockSpec(memory_space=pl.ANY)
    dma = pltpu.SemaphoreType.DMA
    by_chunk = (LEVELS, CHUNKS)
    by_block = (LEVELS, N_ITEM // 2, 2, SHARE, DIM)
    books, final = pl.pallas_call(
        main_kernel,
        out_shape=(pltpu.VMEM(by_block, BF16), pltpu.VMEM(embeddings.shape, BF16)),
        in_specs=[hbm, hbm, hbm],
        out_specs=(vmem, vmem),
        scratch_shapes=[
            pltpu.VMEM(codes.shape, I32),
            pltpu.VMEM(embeddings.shape, BF16),
            pltpu.VMEM((ROWS, LANES), I32),
            pltpu.VMEM((LEVELS, SHARE, DIM), BF16),
            pltpu.VMEM((4, 8, LANES), I32),
            pltpu.VMEM((N_ITEM, 8, LANES), I32),
            pltpu.VMEM((*by_chunk, SLOTS, WIDTH), BF16),
            pltpu.VMEM((*by_chunk, SLOTS, WIDTH), BF16),
            pltpu.VMEM((*by_chunk, SLOTS, WIDTH), BF16),
            pltpu.VMEM((*by_chunk, SLOTS, WIDTH), BF16),
            pltpu.VMEM((*by_chunk, N_ITEM * SHARE, WIDTH), BF16),
            pltpu.VMEM((*by_chunk, N_CENTER * HOP1, WIDTH), BF16),
            pltpu.VMEM((*by_chunk, N_CENTER * HOP1, WIDTH), BF16),
            pltpu.VMEM((LEVELS - 1, CHUNKS, N_CENTER * HOP2, WIDTH), BF16),
            pltpu.VMEM((LEVELS - 1, CHUNKS, N_CENTER * HOP2, WIDTH), BF16),
            pltpu.VMEM((CHUNKS, ITEMS, WIDTH), BF16),
            pltpu.VMEM((ITEMS, ITEMS), BF16),
            pltpu.VMEM((LEVELS, SHARE, SLOTS), BF16),
            pltpu.VMEM((LEVELS, SLOTS, SHARE), BF16),
            pltpu.VMEM((LEVELS, SHARE, LANES), F32),
            pltpu.VMEM((LEVELS, N_CENTER * HOP1, SLOTS), BF16),
            pltpu.VMEM((LEVELS, N_CENTER * HOP2, N_CENTER * HOP1), BF16),
            pltpu.VMEM((LEVELS - 1, SLOTS, N_CENTER * HOP2), BF16),
            dma, dma, dma,
            dma, dma,
            dma(by_chunk), dma(by_chunk),
            dma(by_chunk), dma(by_chunk),
            dma(by_chunk), dma((*by_chunk, 9)), dma(by_chunk),
            dma(by_chunk), dma(by_chunk),
            dma(by_chunk), dma(by_chunk),
            dma((CHUNKS,)), dma((CHUNKS, 9)),
            dma(by_chunk),
        ],
        compiler_params=pltpu.CompilerParams(collective_id=0, has_side_effects=True, vmem_limit_bytes=48 << 20),
    )(codes, embeddings, codebooks)
    books, final = pl.pallas_call(
        copy_kernel,
        out_shape=(jax.ShapeDtypeStruct(by_block, BF16), jax.ShapeDtypeStruct(embeddings.shape, BF16)),
        in_specs=[vmem, vmem],
        out_specs=(hbm, hbm),
        scratch_shapes=[dma((LEVELS + 1,))],
        compiler_params=pltpu.CompilerParams(vmem_limit_bytes=4 << 20),
    )(books, final)
    return books.reshape(codebooks.shape), final


def solution(mesh):
    placed = (P("item", None), P(None, "item"), P(None, "center", None))
    return jax.shard_map(
        per_device,
        mesh=mesh,
        in_specs=placed,
        out_specs=(P(None, "center", None), P("item", None)),
        check_vma=False,
    )
```

```python
import functools

import jax
import jax.numpy as jnp
from jax import lax
from jax.experimental import pallas as pl
from jax.experimental.pallas import tpu as pltpu
from jax.sharding import PartitionSpec as P

MESH = pl.DeviceIdType.MESH
LEVELS, ITEMS, DIM = 3, 2048, 512
N_ITEM, N_CENTER, SHARE, CAP = 16, 8, 128, 32
SLOTS = N_ITEM * CAP
HOP1, HOP2, HOME = 64, 80, ITEMS // N_CENTER
LANES = 128
F32, BF16, I32 = jnp.float32, jnp.bfloat16, jnp.int32


def iota(shape, axis):
    return lax.broadcasted_iota(I32, shape, axis)


def onehot(match):
    return match.astype(F32).astype(BF16)


def dot(a, b):
    return jnp.dot(a, b, preferred_element_type=F32)


ROW_OFF = 0
ROW_D1 = 12
ROW_D2 = 24
ROW_D3 = 36
ROW_POS = 48
ROWS = 64


ARRIVALS = [(0, 0), (3, 0), (1, 0), (0, 1), (3, 1), (1, 1), (2, 0), (2, 1)]


def ordered(cls, n_cls, lower=None):
    a, b = iota((LANES, 2 * LANES), 0), iota((LANES, 2 * LANES), 1)
    before = onehot((b >= LANES) | (a < b))
    member = onehot(iota((n_cls, ITEMS), 0) == cls)
    seen = jnp.zeros((n_cls, LANES), F32)
    ranks = []
    for k in range(ITEMS // LANES):
        part = member[:, k * LANES : (k + 1) * LANES]
        both = dot(part, before)
        ranks.append(jnp.sum(part.astype(F32) * (both[:, :LANES] + seen), axis=0, keepdims=True))
        seen = seen + both[:, LANES:]
    rank = jnp.concatenate(ranks, axis=1).astype(I32)
    if lower is None:
        return rank, None
    r, s = iota((n_cls, n_cls), 0), iota((n_cls, n_cls), 1)
    start = jnp.dot(lower(r, s).astype(F32), seen, precision=lax.Precision.HIGHEST, preferred_element_type=F32)
    start = jnp.concatenate([start] * (ITEMS // LANES), axis=1)
    return rank, jnp.sum(member.astype(F32) * start, axis=0, keepdims=True).astype(I32)


def extract(pos, n_pos, attrs):
    n_hi = n_pos // LANES
    low = onehot(iota((LANES, ITEMS), 0) == jnp.where(pos >= 0, pos & (LANES - 1), -1))
    high = iota((8, ITEMS), 0) == jnp.where(pos >= 0, pos >> 7, -1)
    rows = jnp.concatenate([jnp.where(high, at, 0) for at in attrs], axis=0).astype(F32).astype(BF16)
    got = lax.dot_general(rows, low, (((1,), (1,)), ((), ())), preferred_element_type=F32).astype(I32)
    return [got[8 * k : 8 * k + n_hi] for k in range(len(attrs))]


def slots_of(codes_ref, lev, me):
    code = codes_ref[lev : lev + 1, :]
    block = code >> 7
    rank, _ = ordered(block, N_ITEM * N_CENTER)
    shard = code >> 11
    return shard, code & (SHARE - 1), jnp.where(shard == me, (block & (N_ITEM - 1)) * CAP + rank, -1)


def prepare_codes(idx, lev, off, local):
    idx[ROW_OFF + 4 * lev : ROW_OFF + 4 * lev + 4, :] = extract(local, SLOTS, [off + 1])[0]


def prepare_moves(idx, lev, me, here, local, there, slot_next):
    if lev < LEVELS - 1:
        rank, start = ordered(here * N_CENTER + there, N_CENTER * N_CENTER, lambda r, s: (r // N_CENTER == s // N_CENTER) & (s < r))
        order = rank + start
        via, place = order & 7, order >> 3
        second, _ = ordered(via * N_CENTER + there, N_CENTER * N_CENTER)
        target = [there + 1, second]
        base = HOP2
        pos3 = jnp.where(there == me, via * HOP2 + second, -1)
        slot_next = jnp.maximum(slot_next, 0)
        hi3, lo3 = extract(pos3, N_CENTER * HOP2, [(slot_next >> 8) + 1, slot_next & 255])
        idx[ROW_D3 + 6 * lev : ROW_D3 + 6 * lev + 5, :] = (hi3 - 1) * 256 + lo3
    else:
        rank, start = ordered(here, N_CENTER, lambda r, s: s < r)
        order = rank + start
        via, place = order & 7, rank >> 3
        target = [jnp.ones_like(order), order >> 3]
        base = HOME
        z, h = (via - me) & 3, (via >> 2) != me // 4
        arrival = jnp.zeros_like(via)
        for n, (dz, dh) in enumerate(ARRIVALS):
            arrival = jnp.where((z == dz) & (h == (dh == 1)), n, arrival)
        for k in range(ITEMS // LANES):
            idx[ROW_POS + k : ROW_POS + k + 1, :] = (arrival * HOME + (order >> 3))[:, k * LANES : (k + 1) * LANES]
    via_s, place_s = extract(local, SLOTS, [via + 1, place])
    idx[ROW_D1 + 4 * lev : ROW_D1 + 4 * lev + 4, :] = (via_s - 1) * HOP1 + place_s
    pos2 = jnp.where(via == me, here * HOP1 + place, -1)
    hi2, lo2 = extract(pos2, N_CENTER * HOP1, target)
    idx[ROW_D2 + 4 * lev : ROW_D2 + 4 * lev + 4, :] = (hi2 - 1) * base + lo2


CHUNKS = 2
WIDTH = DIM // CHUNKS
ITEM_OFFSETS = sorted([(y, x, c) for y in range(4) for x in range(2) for c in range(2)][1:], key=lambda o: -(4 * o[1] + min(o[0], 4 - o[0])))
CENTER_OFFSETS = sorted([(h, z) for h in range(2) for z in range(4)][1:], key=lambda o: -(2 * o[0] + min(o[1], 4 - o[1])))


def main_kernel(
    codes_hbm, emb_hbm, cb_ref, books_ref, final_ref,
    codes_ref, emb, idx_ref, cb, meta_s, meta_r, dsend, drecv, rsend, rrecv, book, h1s, h1r, h2s, h2r, frecv, scatter, member, members, total,
    sel1, sel2, sel3,
    codes_sem, emb_sem, cb_sem, meta_ss, meta_rs, d_ss, d_rs, r_ss, r_rs, g_ss, g_rs, p_rs, h1_ss, h1_rs, h2_ss, h2_rs, f_ss, f_rs, out_sem,
):
    item, center = lax.axis_index("item"), lax.axis_index("center")
    my_y, my_x, my_c = item // 4, (item // 2) % 2, item % 2
    my_h, my_z = center // 4, center % 4

    def item_at(y, x, c):
        return ((my_y + y) % 4) * 4 + ((my_x + x) % 2) * 2 + (my_c + c) % 2

    def center_at(h, z):
        return ((my_h + h) % 2) * 4 + (my_z + z) % 4

    def rows(start, size, step):
        return pl.ds(pl.multiple_of(start * step, step), size)

    own_codes = pltpu.make_async_copy(codes_hbm, codes_ref, codes_sem)
    own_codes.start()
    own_emb = pltpu.make_async_copy(emb_hbm, emb, emb_sem)
    own_emb.start()
    barrier = pltpu.get_barrier_semaphore()
    for o in ITEM_OFFSETS:
        pl.semaphore_signal(barrier, inc=1, device_id=(item_at(*o), center), device_id_type=MESH)
    for o in CENTER_OFFSETS:
        pl.semaphore_signal(barrier, inc=1, device_id=(item, center_at(*o)), device_id_type=MESH)

    own_cb = pltpu.make_async_copy(cb_ref.at[:, rows(item, SHARE, SHARE), :], cb, cb_sem)
    own_cb.start()

    def remote(src, dst, ss, rs, to):
        return pltpu.make_async_remote_copy(
            src_ref=src, dst_ref=dst, send_sem=ss, recv_sem=rs, device_id=to, device_id_type=MESH
        )

    def send(src, dst, ss, rs, to):
        cp = remote(src, dst, ss, rs, to)
        cp.start()
        return cp

    def whole(ref, ss, rs):
        return remote(ref, ref, ss, rs, (item, center))

    pending = []

    own_codes.wait()
    known = [slots_of(codes_ref, 0, center)]
    for k in range(ITEMS // LANES):
        row = known[0][2][:, k * LANES : (k + 1) * LANES]
        scatter[0:SLOTS, k * LANES : (k + 1) * LANES] = onehot(iota((SLOTS, LANES), 0) == row)
    own_emb.wait()

    def send_metas():
        for lev in range(1, LEVELS):
            known.append(slots_of(codes_ref, lev, center))
        for lev in range(LEVELS):
            prepare_codes(idx_ref, lev, *known[lev][1:])
        meta_s[...] = jnp.zeros_like(meta_s)
        for h in range(4):
            for lev in range(LEVELS):
                meta_s[h, lev : lev + 1, :] = idx_ref[ROW_OFF + 4 * lev + h : ROW_OFF + 4 * lev + h + 1, :]
        for o in ITEM_OFFSETS:
            to = item_at(*o)
            send(meta_s.at[to // 4], meta_r.at[item], meta_ss, meta_rs, (to, center))
        meta_r[item] = meta_s[item // 4]
        pending.append(whole(meta_r.at[pl.ds(0, 15)], meta_ss, meta_rs))

    def selection(ref, first, n_in, n_out):
        for k in range(n_in // LANES):
            ref[0:n_out, k * LANES : (k + 1) * LANES] = onehot(
                iota((n_out, LANES), 0) == idx_ref[first + k : first + k + 1, :]
            )

    def select(ref, n_in, n_out, source):
        return dot(ref[0:n_out, 0:n_in], source).astype(BF16)

    def receive_metas():
        whole(meta_r.at[pl.ds(0, 15)], meta_ss, meta_rs).wait_recv()
        own_cb.wait()
        lane = iota((8, LANES), 1)
        mine = (lane >= (item % 4) * CAP) & (lane < (item % 4 + 1) * CAP)
        for q in range(4):
            codes = jnp.zeros((8, LANES), I32)
            for j in range(4):
                piece = jnp.where(mine, meta_r[4 * q + j], 0)
                codes = codes + pltpu.roll(piece, ((j + 4 - item % 4) % 4) * CAP, 1)
            for lev in range(LEVELS):
                part = (iota((SHARE, LANES), 0) + 1 == codes[lev : lev + 1, :]).astype(F32)
                member[lev, :, q * LANES : (q + 1) * LANES] = part.astype(BF16)
                members[lev, q * LANES : (q + 1) * LANES, :] = part.T.astype(BF16)
        for lev in range(LEVELS):
            count = jnp.sum(member[lev].astype(F32), axis=1, keepdims=True)
            total[lev] = jnp.broadcast_to(count + 1.0, (SHARE, LANES))

    def moves(lev):
        nxt = known[min(lev + 1, LEVELS - 1)]
        prepare_moves(idx_ref, lev, center, known[lev][0], known[lev][2], nxt[0], nxt[2])

    def first_selection(lev):
        selection(sel1.at[lev], ROW_D1 + 4 * lev, SLOTS, N_CENTER * HOP1)

    def second_selection(lev):
        selection(sel2.at[lev], ROW_D2 + 4 * lev, N_CENTER * HOP1, N_CENTER * HOP2 if lev < LEVELS - 1 else HOME)

    def third_selection(lev):
        selection(sel3.at[lev], ROW_D3 + 6 * lev, N_CENTER * HOP2, SLOTS)

    def build_scatter(n):
        for k in range(3 * n, min(3 * n + 3, ITEMS // LANES)):
            row = jnp.broadcast_to(idx_ref[ROW_POS + k : ROW_POS + k + 1, :].astype(F32), (LANES, LANES))
            col = row.T.astype(I32)
            for g in range(ITEMS // LANES):
                scatter[k * LANES : (k + 1) * LANES, g * LANES : (g + 1) * LANES] = onehot(
                    iota((LANES, LANES), 1) + g * LANES == col
                )

    def mover(buf, size, ring, ss, rs):
        def move(n, at, to, part=None):
            index = ring(*at)[0]
            if part is None:
                piece = buf.at[rows(index, size, size)]
            else:
                piece = buf.at[rows(index * 2 + part, size // 2, size // 2)]
            return send(piece, piece, ss, rs.at[n], ring(*to)[1])

        return move

    own, up, down, over = (0, 0), (1, 0), (3, 0), (0, 1)

    def gather_rows(k):
        move = mover(frecv.at[k], HOME, lambda z, h: (center_at(h, z), (item, center_at(h, z))), f_ss.at[k], f_rs.at[k])
        first = [move(0, own, up), move(1, own, down), move(2, own, over)]
        yield
        first[0].wait_recv()
        a = move(3, down, up, 0)
        first[1].wait_recv()
        d = move(4, up, down, 1)
        first[2].wait_recv()
        rest = [move(5, over, up), move(6, over, down)]
        yield
        a.wait_recv()
        rest.append(move(7, (2, 0), over, 0))
        d.wait_recv()
        rest.append(move(8, (2, 0), over, 1))
        yield
        for cp in rest:
            cp.wait_recv()

    def gather_books(lev, k):
        bk, cols = book.at[lev, k], slice(k * WIDTH, (k + 1) * WIDTH)
        move = mover(
            bk, SHARE,
            lambda y, x: (my_c * 8 + item_at(y, x, 0) // 2, (item_at(y, x, 0), center)),
            g_ss.at[lev, k], g_rs.at[lev, k],
        )
        first = [move(0, own, up), move(1, own, down), move(2, own, over)]
        yield
        for cp in first:
            cp.wait_recv()
        second = [move(3, down, up, 0), move(4, up, down, 1), move(5, over, up), move(6, over, down)]
        yield
        second[2].wait_recv()
        third = [move(7, (3, 1), up, 0)]
        second[3].wait_recv()
        third.append(move(8, (1, 1), down, 1))
        yield
        for cp in second[:2] + third:
            cp.wait_recv()
        half = bk.at[rows(my_c, 8 * SHARE, 8 * SHARE)]
        passed = send(half, half, g_ss.at[lev, k], p_rs.at[lev, k], (item_at(0, 0, 1), center))
        yield
        passed.wait_recv()
        for c in range(2):
            for q in range(8):
                pltpu.make_async_copy(
                    bk.at[pl.ds((c * 8 + q) * SHARE, SHARE)], books_ref.at[lev, q, c, :, cols], out_sem.at[lev, k]
                ).start()
        pending.append(whole(bk.at[pl.ds(0, 15 * SHARE)], g_ss.at[lev, k], p_rs.at[lev, k]))

    def exchange(src, dst, size, ss, rs):
        own = rows(center, size, size)
        for o in CENTER_OFFSETS:
            to = center_at(*o)
            send(src.at[rows(to, size, size)], dst.at[own], ss, rs, (item, to))
        dst[own, :] = src[own, :]
        cp = whole(dst.at[pl.ds(0, 7 * size)], ss, rs)
        pending.append(cp)
        return cp

    def place(k, cols, part):
        blocks = [frecv[k, rows(center_at(h, z), HOME, HOME), :] for z, h in ARRIVALS[4 * part : 4 * part + 4]]
        source = jnp.concatenate(blocks, axis=0)
        for t in range(ITEMS // 256):
            at = slice(t * 256, (t + 1) * 256)
            found = dot(scatter[at, 4 * part * HOME : 4 * (part + 1) * HOME], source).astype(BF16)
            final_ref[at, cols] = found if part == 0 else final_ref[at, cols] + found

    def swap(src, dst, ss, rs):
        own_rows = rows(item, CAP, CAP)
        for o in ITEM_OFFSETS:
            to = item_at(*o)
            send(src.at[rows(to, CAP, CAP)], dst.at[own_rows], ss, rs, (to, center))
        dst[own_rows, :] = src[own_rows, :]
        cp = whole(dst.at[pl.ds(0, 15 * CAP)], ss, rs)
        pending.append(cp)
        return cp

    def do(f, *args):
        return lambda: f(*args)

    chores = [
        [send_metas, do(moves, 0)],
        [do(first_selection, 0), do(second_selection, 0)],
        [do(third_selection, 0), do(moves, 1)],
        [do(first_selection, 1), do(second_selection, 1)],
        [do(third_selection, 1)],
        [do(moves, 2)],
        [do(first_selection, 2), do(second_selection, 2)],
        [do(build_scatter, 0)],
        [do(build_scatter, 1)],
        [do(build_scatter, 2)],
        [do(build_scatter, 3)],
        [do(build_scatter, 4)],
        [do(build_scatter, 5)],
        [],
    ]

    def program(k):
        cols = slice(k * WIDTH, (k + 1) * WIDTH)
        last = k == CHUNKS - 1
        background = []

        def idle():
            if last:
                for chore in chores.pop(0):
                    chore()

        def step():
            background[:] = [g for g in background if next(g, 0) is None]

        dsend[0, k] = dot(scatter[0:SLOTS, :], emb[:, cols]).astype(BF16)
        if k == 0:
            pl.semaphore_wait(barrier, len(ITEM_OFFSETS) + len(CENTER_OFFSETS))
        for lev in range(LEVELS):
            arrived = swap(dsend.at[lev, k], drecv.at[lev, k], d_ss.at[lev, k], d_rs.at[lev, k])
            step()
            idle()
            yield
            if lev == 0 and k == 0:
                receive_metas()
            arrived.wait_recv()
            pooled = dot(member[lev], drecv[lev, k])
            size = jnp.concatenate([total[lev]] * (WIDTH // LANES), axis=1)
            updated = ((pooled + cb[lev, :, cols].astype(F32)) / size).astype(BF16)
            rsend[lev, k] = (drecv[lev, k].astype(F32) - dot(members[lev], updated)).astype(BF16)
            arrived = swap(rsend.at[lev, k], rrecv.at[lev, k], r_ss.at[lev, k], r_rs.at[lev, k])
            book[lev, k, rows(my_c * 8 + item // 2, SHARE, SHARE), :] = updated
            step()
            fresh = gather_books(lev, k)
            idle()
            yield
            arrived.wait_recv()
            h1s[lev, k] = select(sel1.at[lev], SLOTS, N_CENTER * HOP1, rrecv[lev, k])
            hop = exchange(h1s.at[lev, k], h1r.at[lev, k], HOP1, h1_ss.at[lev, k], h1_rs.at[lev, k])
            step()
            background.append(fresh)
            next(fresh)
            idle()
            yield
            hop.wait_recv()
            if lev < LEVELS - 1:
                h2s[lev, k] = select(sel2.at[lev], N_CENTER * HOP1, N_CENTER * HOP2, h1r[lev, k])
                hop = exchange(h2s.at[lev, k], h2r.at[lev, k], HOP2, h2_ss.at[lev, k], h2_rs.at[lev, k])
                step()
                idle()
                yield
                hop.wait_recv()
                dsend[lev + 1, k] = select(sel3.at[lev], N_CENTER * HOP2, SLOTS, h2r[lev, k])
            else:
                frecv[k, rows(center, HOME, HOME), :] = select(sel2.at[lev], N_CENTER * HOP1, HOME, h1r[lev, k])
                phases = gather_rows(k)
                for phase in range(3):
                    next(phases)
                    step()
                    idle()
                    if phase == 2:
                        place(k, cols, 0)
                    yield
                next(phases, 0)
                while background:
                    step()
                place(k, cols, 1)
                pending.append(whole(frecv.at[k, pl.ds(0, 7 * HOME)], f_ss.at[k], f_rs.at[k, 0]))

    running = [program(k) for k in range(CHUNKS)]
    while running:
        running = [p for p in running if next(p, 0) is None]

    for lev in range(LEVELS):
        for k in range(CHUNKS):
            pltpu.make_async_copy(book.at[lev, k], book.at[lev, k], out_sem.at[lev, k]).wait()
    for cp in pending:
        cp.wait_send()


def copy_kernel(a_ref, b_ref, oa_ref, ob_ref, sem):
    pairs = [(b_ref.at[pl.ds(h * 512, 512)], ob_ref.at[pl.ds(h * 512, 512)]) for h in range(4)]
    pairs += [(a_ref.at[lev, q], oa_ref.at[lev, q]) for lev in range(LEVELS) for q in range(N_ITEM // 2)]
    cps = [pltpu.make_async_copy(src, dst, sem.at[n]) for n, (src, dst) in enumerate(pairs)]
    for cp in cps:
        cp.start()
    for cp in cps:
        cp.wait()


def per_device(embeddings, codes, codebooks):
    vmem = pl.BlockSpec(memory_space=pltpu.VMEM)
    hbm = pl.BlockSpec(memory_space=pl.ANY)
    dma = pltpu.SemaphoreType.DMA
    by_chunk = (LEVELS, CHUNKS)
    by_block = (LEVELS, N_ITEM // 2, 2, SHARE, DIM)
    books, final = pl.pallas_call(
        main_kernel,
        out_shape=(pltpu.VMEM(by_block, BF16), pltpu.VMEM(embeddings.shape, BF16)),
        in_specs=[hbm, hbm, hbm],
        out_specs=(vmem, vmem),
        scratch_shapes=[
            pltpu.VMEM(codes.shape, I32),
            pltpu.VMEM(embeddings.shape, BF16),
            pltpu.VMEM((ROWS, LANES), I32),
            pltpu.VMEM((LEVELS, SHARE, DIM), BF16),
            pltpu.VMEM((4, 8, LANES), I32),
            pltpu.VMEM((N_ITEM, 8, LANES), I32),
            pltpu.VMEM((*by_chunk, SLOTS, WIDTH), BF16),
            pltpu.VMEM((*by_chunk, SLOTS, WIDTH), BF16),
            pltpu.VMEM((*by_chunk, SLOTS, WIDTH), BF16),
            pltpu.VMEM((*by_chunk, SLOTS, WIDTH), BF16),
            pltpu.VMEM((*by_chunk, N_ITEM * SHARE, WIDTH), BF16),
            pltpu.VMEM((*by_chunk, N_CENTER * HOP1, WIDTH), BF16),
            pltpu.VMEM((*by_chunk, N_CENTER * HOP1, WIDTH), BF16),
            pltpu.VMEM((LEVELS - 1, CHUNKS, N_CENTER * HOP2, WIDTH), BF16),
            pltpu.VMEM((LEVELS - 1, CHUNKS, N_CENTER * HOP2, WIDTH), BF16),
            pltpu.VMEM((CHUNKS, ITEMS, WIDTH), BF16),
            pltpu.VMEM((ITEMS, ITEMS), BF16),
            pltpu.VMEM((LEVELS, SHARE, SLOTS), BF16),
            pltpu.VMEM((LEVELS, SLOTS, SHARE), BF16),
            pltpu.VMEM((LEVELS, SHARE, LANES), F32),
            pltpu.VMEM((LEVELS, N_CENTER * HOP1, SLOTS), BF16),
            pltpu.VMEM((LEVELS, N_CENTER * HOP2, N_CENTER * HOP1), BF16),
            pltpu.VMEM((LEVELS - 1, SLOTS, N_CENTER * HOP2), BF16),
            dma, dma, dma,
            dma, dma,
            dma(by_chunk), dma(by_chunk),
            dma(by_chunk), dma(by_chunk),
            dma(by_chunk), dma((*by_chunk, 9)), dma(by_chunk),
            dma(by_chunk), dma(by_chunk),
            dma(by_chunk), dma(by_chunk),
            dma((CHUNKS,)), dma((CHUNKS, 9)),
            dma(by_chunk),
        ],
        compiler_params=pltpu.CompilerParams(collective_id=0, has_side_effects=True, vmem_limit_bytes=48 << 20),
    )(codes, embeddings, codebooks)
    books, final = pl.pallas_call(
        copy_kernel,
        out_shape=(jax.ShapeDtypeStruct(by_block, BF16), jax.ShapeDtypeStruct(embeddings.shape, BF16)),
        in_specs=[vmem, vmem],
        out_specs=(hbm, hbm),
        scratch_shapes=[dma((4 + LEVELS * N_ITEM // 2,))],
        compiler_params=pltpu.CompilerParams(vmem_limit_bytes=4 << 20),
    )(books, final)
    return books.reshape(codebooks.shape), final


def solution(mesh):
    placed = (P("item", None), P(None, "item"), P(None, "center", None))
    return jax.shard_map(
        per_device,
        mesh=mesh,
        in_specs=placed,
        out_specs=(P(None, "center", None), P("item", None)),
        check_vma=False,
    )
```

```python
import functools

import jax
import jax.numpy as jnp
from jax import lax
from jax.experimental import pallas as pl
from jax.experimental.pallas import tpu as pltpu
from jax.sharding import PartitionSpec as P

MESH = pl.DeviceIdType.MESH
LEVELS, ITEMS, DIM = 3, 2048, 512
N_ITEM, N_CENTER, SHARE, CAP = 16, 8, 128, 32
SLOTS = N_ITEM * CAP
HOP1, HOP2, HOME = 64, 80, ITEMS // N_CENTER
LANES = 128
F32, BF16, I32 = jnp.float32, jnp.bfloat16, jnp.int32


def iota(shape, axis):
    return lax.broadcasted_iota(I32, shape, axis)


def onehot(match):
    return match.astype(F32).astype(BF16)


def dot(a, b):
    return jnp.dot(a, b, preferred_element_type=F32)


ROW_OFF = 0
ROW_D1 = 12
ROW_D2 = 24
ROW_D3 = 36
ROW_POS = 48
ROWS = 64


ARRIVALS = [(0, 0), (3, 0), (1, 0), (0, 1), (3, 1), (1, 1), (2, 0), (2, 1)]


def ordered(cls, n_cls, lower=None):
    a, b = iota((LANES, 2 * LANES), 0), iota((LANES, 2 * LANES), 1)
    before = onehot((b >= LANES) | (a < b))
    member = onehot(iota((n_cls, ITEMS), 0) == cls)
    seen = jnp.zeros((n_cls, LANES), F32)
    ranks = []
    for k in range(ITEMS // LANES):
        part = member[:, k * LANES : (k + 1) * LANES]
        both = dot(part, before)
        ranks.append(jnp.sum(part.astype(F32) * (both[:, :LANES] + seen), axis=0, keepdims=True))
        seen = seen + both[:, LANES:]
    rank = jnp.concatenate(ranks, axis=1).astype(I32)
    if lower is None:
        return rank, None
    r, s = iota((n_cls, n_cls), 0), iota((n_cls, n_cls), 1)
    start = jnp.dot(lower(r, s).astype(F32), seen, precision=lax.Precision.HIGHEST, preferred_element_type=F32)
    start = jnp.concatenate([start] * (ITEMS // LANES), axis=1)
    return rank, jnp.sum(member.astype(F32) * start, axis=0, keepdims=True).astype(I32)


def extract(pos, n_pos, attrs):
    n_hi = n_pos // LANES
    low = onehot(iota((LANES, ITEMS), 0) == jnp.where(pos >= 0, pos & (LANES - 1), -1))
    high = iota((8, ITEMS), 0) == jnp.where(pos >= 0, pos >> 7, -1)
    rows = jnp.concatenate([jnp.where(high, at, 0) for at in attrs], axis=0).astype(F32).astype(BF16)
    got = lax.dot_general(rows, low, (((1,), (1,)), ((), ())), preferred_element_type=F32).astype(I32)
    return [got[8 * k : 8 * k + n_hi] for k in range(len(attrs))]


def slots_of(codes_ref, lev, me):
    code = codes_ref[lev : lev + 1, :]
    block = code >> 7
    rank, _ = ordered(block, N_ITEM * N_CENTER)
    shard = code >> 11
    return shard, code & (SHARE - 1), jnp.where(shard == me, (block & (N_ITEM - 1)) * CAP + rank, -1)


def prepare_codes(idx, lev, off, local):
    idx[ROW_OFF + 4 * lev : ROW_OFF + 4 * lev + 4, :] = extract(local, SLOTS, [off + 1])[0]


def prepare_moves(idx, lev, me, here, local, there, slot_next):
    if lev < LEVELS - 1:
        rank, start = ordered(here * N_CENTER + there, N_CENTER * N_CENTER, lambda r, s: (r // N_CENTER == s // N_CENTER) & (s < r))
        order = rank + start
        via, place = order & 7, order >> 3
        second, _ = ordered(via * N_CENTER + there, N_CENTER * N_CENTER)
        target = [there + 1, second]
        base = HOP2
        pos3 = jnp.where(there == me, via * HOP2 + second, -1)
        slot_next = jnp.maximum(slot_next, 0)
        hi3, lo3 = extract(pos3, N_CENTER * HOP2, [(slot_next >> 8) + 1, slot_next & 255])
        idx[ROW_D3 + 6 * lev : ROW_D3 + 6 * lev + 5, :] = (hi3 - 1) * 256 + lo3
    else:
        rank, start = ordered(here, N_CENTER, lambda r, s: s < r)
        order = rank + start
        via, place = order & 7, rank >> 3
        target = [jnp.ones_like(order), order >> 3]
        base = HOME
        z, h = (via - me) & 3, (via >> 2) != me // 4
        arrival = jnp.zeros_like(via)
        for n, (dz, dh) in enumerate(ARRIVALS):
            arrival = jnp.where((z == dz) & (h == (dh == 1)), n, arrival)
        for k in range(ITEMS // LANES):
            idx[ROW_POS + k : ROW_POS + k + 1, :] = (arrival * HOME + (order >> 3))[:, k * LANES : (k + 1) * LANES]
    via_s, place_s = extract(local, SLOTS, [via + 1, place])
    idx[ROW_D1 + 4 * lev : ROW_D1 + 4 * lev + 4, :] = (via_s - 1) * HOP1 + place_s
    pos2 = jnp.where(via == me, here * HOP1 + place, -1)
    hi2, lo2 = extract(pos2, N_CENTER * HOP1, target)
    idx[ROW_D2 + 4 * lev : ROW_D2 + 4 * lev + 4, :] = (hi2 - 1) * base + lo2


CHUNKS = 2
TILE = 64
WIDTH = DIM // CHUNKS
ITEM_OFFSETS = sorted([(y, x, c) for y in range(4) for x in range(2) for c in range(2)][1:], key=lambda o: -(4 * o[1] + min(o[0], 4 - o[0])))
CENTER_OFFSETS = sorted([(h, z) for h in range(2) for z in range(4)][1:], key=lambda o: -(2 * o[0] + min(o[1], 4 - o[1])))


def main_kernel(
    codes_hbm, emb_hbm, cb_ref, books_ref, final_ref,
    codes_ref, emb, idx_ref, cb, meta_s, meta_r, dsend, drecv, rsend, rrecv, book, h1s, h1r, h2s, h2r, frecv, scatter, member, members, total,
    sel1, sel2, sel3,
    codes_sem, emb_sem, cb_sem, meta_ss, meta_rs, d_ss, d_rs, r_ss, r_rs, g_ss, g_rs, p_rs, h1_ss, h1_rs, h2_ss, h2_rs, f_ss, f_rs, out_sem,
):
    item, center = lax.axis_index("item"), lax.axis_index("center")
    my_y, my_x, my_c = item // 4, (item // 2) % 2, item % 2
    my_h, my_z = center // 4, center % 4

    def item_at(y, x, c):
        return ((my_y + y) % 4) * 4 + ((my_x + x) % 2) * 2 + (my_c + c) % 2

    def center_at(h, z):
        return ((my_h + h) % 2) * 4 + (my_z + z) % 4

    def rows(start, size, step):
        return pl.ds(pl.multiple_of(start * step, step), size)

    own_codes = pltpu.make_async_copy(codes_hbm, codes_ref, codes_sem)
    own_codes.start()
    own_emb = pltpu.make_async_copy(emb_hbm, emb, emb_sem)
    own_emb.start()
    barrier = pltpu.get_barrier_semaphore()
    for o in ITEM_OFFSETS:
        pl.semaphore_signal(barrier, inc=1, device_id=(item_at(*o), center), device_id_type=MESH)
    for o in CENTER_OFFSETS:
        pl.semaphore_signal(barrier, inc=1, device_id=(item, center_at(*o)), device_id_type=MESH)

    own_cb = pltpu.make_async_copy(cb_ref.at[:, rows(item, SHARE, SHARE), :], cb, cb_sem)
    own_cb.start()

    def remote(src, dst, ss, rs, to):
        return pltpu.make_async_remote_copy(
            src_ref=src, dst_ref=dst, send_sem=ss, recv_sem=rs, device_id=to, device_id_type=MESH
        )

    def send(src, dst, ss, rs, to):
        cp = remote(src, dst, ss, rs, to)
        cp.start()
        return cp

    def whole(ref, ss, rs):
        return remote(ref, ref, ss, rs, (item, center))

    pending = []

    own_codes.wait()
    known = [slots_of(codes_ref, 0, center)]
    for k in range(ITEMS // LANES):
        idx_ref[ROW_POS + k : ROW_POS + k + 1, :] = known[0][2][:, k * LANES : (k + 1) * LANES]

    @pl.loop(0, SLOTS // TILE)
    def _(t):
        at = pl.multiple_of(t * TILE, TILE)
        for k in range(ITEMS // LANES):
            scatter[pl.ds(at, TILE), k * LANES : (k + 1) * LANES] = onehot(
                iota((TILE, LANES), 0) + at == idx_ref[ROW_POS + k : ROW_POS + k + 1, :]
            )

    own_emb.wait()

    def send_metas():
        for lev in range(1, LEVELS):
            known.append(slots_of(codes_ref, lev, center))
        for lev in range(LEVELS):
            prepare_codes(idx_ref, lev, *known[lev][1:])
        meta_s[...] = jnp.zeros_like(meta_s)
        for h in range(4):
            for lev in range(LEVELS):
                meta_s[h, lev : lev + 1, :] = idx_ref[ROW_OFF + 4 * lev + h : ROW_OFF + 4 * lev + h + 1, :]
        for o in ITEM_OFFSETS:
            to = item_at(*o)
            send(meta_s.at[to // 4], meta_r.at[item], meta_ss, meta_rs, (to, center))
        meta_r[item] = meta_s[item // 4]
        pending.append(whole(meta_r.at[pl.ds(0, 15)], meta_ss, meta_rs))

    def selection(ref, first, n_in, n_out):
        @pl.loop(0, n_out // TILE)
        def _(t):
            at = pl.multiple_of(t * TILE, TILE)
            for k in range(n_in // LANES):
                ref[pl.ds(at, TILE), k * LANES : (k + 1) * LANES] = onehot(
                    iota((TILE, LANES), 0) + at == idx_ref[first + k : first + k + 1, :]
                )

    def select(ref, n_in, n_out, source):
        return dot(ref[0:n_out, 0:n_in], source).astype(BF16)

    def receive_metas():
        whole(meta_r.at[pl.ds(0, 15)], meta_ss, meta_rs).wait_recv()
        own_cb.wait()
        lane = iota((8, LANES), 1)
        mine = (lane >= (item % 4) * CAP) & (lane < (item % 4 + 1) * CAP)
        for q in range(4):
            codes = jnp.zeros((8, LANES), I32)
            for j in range(4):
                piece = jnp.where(mine, meta_r[4 * q + j], 0)
                codes = codes + pltpu.roll(piece, ((j + 4 - item % 4) % 4) * CAP, 1)
            for lev in range(LEVELS):
                part = (iota((SHARE, LANES), 0) + 1 == codes[lev : lev + 1, :]).astype(F32)
                member[lev, :, q * LANES : (q + 1) * LANES] = part.astype(BF16)
                members[lev, q * LANES : (q + 1) * LANES, :] = part.T.astype(BF16)
        for lev in range(LEVELS):
            count = jnp.sum(member[lev].astype(F32), axis=1, keepdims=True)
            total[lev] = jnp.broadcast_to(count + 1.0, (SHARE, LANES))

    def moves(lev):
        nxt = known[min(lev + 1, LEVELS - 1)]
        prepare_moves(idx_ref, lev, center, known[lev][0], known[lev][2], nxt[0], nxt[2])

    def first_selection(lev):
        selection(sel1.at[lev], ROW_D1 + 4 * lev, SLOTS, N_CENTER * HOP1)

    def second_selection(lev):
        selection(sel2.at[lev], ROW_D2 + 4 * lev, N_CENTER * HOP1, N_CENTER * HOP2 if lev < LEVELS - 1 else HOME)

    def third_selection(lev):
        selection(sel3.at[lev], ROW_D3 + 6 * lev, N_CENTER * HOP2, SLOTS)

    def build_scatter(n):
        @pl.loop(3 * n, min(3 * n + 3, ITEMS // LANES))
        def _(k):
            row = jnp.broadcast_to(idx_ref[pl.ds(ROW_POS + k, 1), :].astype(F32), (LANES, LANES))
            col = row.T.astype(I32)
            at = pl.ds(pl.multiple_of(k * LANES, LANES), LANES)
            for g in range(ITEMS // LANES):
                scatter[at, g * LANES : (g + 1) * LANES] = onehot(iota((LANES, LANES), 1) + g * LANES == col)

    def mover(buf, size, ring, ss, rs):
        def move(n, at, to, part=None):
            index = ring(*at)[0]
            if part is None:
                piece = buf.at[rows(index, size, size)]
            else:
                piece = buf.at[rows(index * 2 + part, size // 2, size // 2)]
            return send(piece, piece, ss, rs.at[n], ring(*to)[1])

        return move

    own, up, down, over = (0, 0), (1, 0), (3, 0), (0, 1)

    def gather_rows(k):
        move = mover(frecv.at[k], HOME, lambda z, h: (center_at(h, z), (item, center_at(h, z))), f_ss.at[k], f_rs.at[k])
        first = [move(0, own, up), move(1, own, down), move(2, own, over)]
        yield
        first[0].wait_recv()
        a = move(3, down, up, 0)
        first[1].wait_recv()
        d = move(4, up, down, 1)
        first[2].wait_recv()
        rest = [move(5, over, up), move(6, over, down)]
        yield
        a.wait_recv()
        rest.append(move(7, (2, 0), over, 0))
        d.wait_recv()
        rest.append(move(8, (2, 0), over, 1))
        yield
        for cp in rest:
            cp.wait_recv()

    def gather_books(lev, k):
        bk, cols = book.at[lev, k], slice(k * WIDTH, (k + 1) * WIDTH)
        move = mover(
            bk, SHARE,
            lambda y, x: (my_c * 8 + item_at(y, x, 0) // 2, (item_at(y, x, 0), center)),
            g_ss.at[lev, k], g_rs.at[lev, k],
        )
        first = [move(0, own, up), move(1, own, down), move(2, own, over)]
        yield
        for cp in first:
            cp.wait_recv()
        second = [move(3, down, up, 0), move(4, up, down, 1), move(5, over, up), move(6, over, down)]
        yield
        second[2].wait_recv()
        third = [move(7, (3, 1), up, 0)]
        second[3].wait_recv()
        third.append(move(8, (1, 1), down, 1))
        yield
        for cp in second[:2] + third:
            cp.wait_recv()
        half = bk.at[rows(my_c, 8 * SHARE, 8 * SHARE)]
        passed = send(half, half, g_ss.at[lev, k], p_rs.at[lev, k], (item_at(0, 0, 1), center))
        yield
        passed.wait_recv()
        for c in range(2):
            for q in range(8):
                pltpu.make_async_copy(
                    bk.at[pl.ds((c * 8 + q) * SHARE, SHARE)], books_ref.at[lev, q, c, :, cols], out_sem.at[lev, k]
                ).start()
        pending.append(whole(bk.at[pl.ds(0, 15 * SHARE)], g_ss.at[lev, k], p_rs.at[lev, k]))

    def exchange(src, dst, size, ss, rs):
        own = rows(center, size, size)
        for o in CENTER_OFFSETS:
            to = center_at(*o)
            send(src.at[rows(to, size, size)], dst.at[own], ss, rs, (item, to))
        dst[own, :] = src[own, :]
        cp = whole(dst.at[pl.ds(0, 7 * size)], ss, rs)
        pending.append(cp)
        return cp

    def place(k, cols, part):
        blocks = [frecv[k, rows(center_at(h, z), HOME, HOME), :] for z, h in ARRIVALS[4 * part : 4 * part + 4]]
        source = jnp.concatenate(blocks, axis=0)
        for t in range(ITEMS // 256):
            at = slice(t * 256, (t + 1) * 256)
            found = dot(scatter[at, 4 * part * HOME : 4 * (part + 1) * HOME], source).astype(BF16)
            final_ref[at, cols] = found if part == 0 else final_ref[at, cols] + found

    def swap(src, dst, ss, rs):
        own_rows = rows(item, CAP, CAP)
        for o in ITEM_OFFSETS:
            to = item_at(*o)
            send(src.at[rows(to, CAP, CAP)], dst.at[own_rows], ss, rs, (to, center))
        dst[own_rows, :] = src[own_rows, :]
        cp = whole(dst.at[pl.ds(0, 15 * CAP)], ss, rs)
        pending.append(cp)
        return cp

    def do(f, *args):
        return lambda: f(*args)

    chores = [
        [send_metas, do(moves, 0)],
        [do(first_selection, 0), do(second_selection, 0)],
        [do(third_selection, 0), do(moves, 1)],
        [do(first_selection, 1), do(second_selection, 1)],
        [do(third_selection, 1)],
        [do(moves, 2)],
        [do(first_selection, 2), do(second_selection, 2)],
        [do(build_scatter, 0)],
        [do(build_scatter, 1)],
        [do(build_scatter, 2)],
        [do(build_scatter, 3)],
        [do(build_scatter, 4)],
        [do(build_scatter, 5)],
        [],
    ]

    def program(k):
        cols = slice(k * WIDTH, (k + 1) * WIDTH)
        last = k == CHUNKS - 1
        background = []

        def idle():
            if last:
                for chore in chores.pop(0):
                    chore()

        def step():
            background[:] = [g for g in background if next(g, 0) is None]

        dsend[0, k] = dot(scatter[0:SLOTS, :], emb[:, cols]).astype(BF16)
        if k == 0:
            pl.semaphore_wait(barrier, len(ITEM_OFFSETS) + len(CENTER_OFFSETS))
        for lev in range(LEVELS):
            arrived = swap(dsend.at[lev, k], drecv.at[lev, k], d_ss.at[lev, k], d_rs.at[lev, k])
            step()
            idle()
            yield
            if lev == 0 and k == 0:
                receive_metas()
            arrived.wait_recv()
            pooled = dot(member[lev], drecv[lev, k])
            size = jnp.concatenate([total[lev]] * (WIDTH // LANES), axis=1)
            updated = ((pooled + cb[lev, :, cols].astype(F32)) / size).astype(BF16)
            rsend[lev, k] = (drecv[lev, k].astype(F32) - dot(members[lev], updated)).astype(BF16)
            arrived = swap(rsend.at[lev, k], rrecv.at[lev, k], r_ss.at[lev, k], r_rs.at[lev, k])
            book[lev, k, rows(my_c * 8 + item // 2, SHARE, SHARE), :] = updated
            step()
            fresh = gather_books(lev, k)
            idle()
            yield
            arrived.wait_recv()
            h1s[lev, k] = select(sel1.at[lev], SLOTS, N_CENTER * HOP1, rrecv[lev, k])
            hop = exchange(h1s.at[lev, k], h1r.at[lev, k], HOP1, h1_ss.at[lev, k], h1_rs.at[lev, k])
            step()
            background.append(fresh)
            next(fresh)
            idle()
            yield
            hop.wait_recv()
            if lev < LEVELS - 1:
                h2s[lev, k] = select(sel2.at[lev], N_CENTER * HOP1, N_CENTER * HOP2, h1r[lev, k])
                hop = exchange(h2s.at[lev, k], h2r.at[lev, k], HOP2, h2_ss.at[lev, k], h2_rs.at[lev, k])
                step()
                idle()
                yield
                hop.wait_recv()
                dsend[lev + 1, k] = select(sel3.at[lev], N_CENTER * HOP2, SLOTS, h2r[lev, k])
            else:
                frecv[k, rows(center, HOME, HOME), :] = select(sel2.at[lev], N_CENTER * HOP1, HOME, h1r[lev, k])
                phases = gather_rows(k)
                for phase in range(3):
                    next(phases)
                    step()
                    idle()
                    if phase == 2:
                        place(k, cols, 0)
                    yield
                next(phases, 0)
                while background:
                    step()
                place(k, cols, 1)
                pending.append(whole(frecv.at[k, pl.ds(0, 7 * HOME)], f_ss.at[k], f_rs.at[k, 0]))

    running = [program(k) for k in range(CHUNKS)]
    while running:
        running = [p for p in running if next(p, 0) is None]

    for lev in range(LEVELS):
        for k in range(CHUNKS):
            pltpu.make_async_copy(book.at[lev, k], book.at[lev, k], out_sem.at[lev, k]).wait()
    for cp in pending:
        cp.wait_send()


def copy_kernel(a_ref, b_ref, oa_ref, ob_ref, sem):
    pairs = [(b_ref.at[pl.ds(h * 512, 512)], ob_ref.at[pl.ds(h * 512, 512)]) for h in range(4)]
    pairs += [(a_ref.at[lev, q], oa_ref.at[lev, q]) for lev in range(LEVELS) for q in range(N_ITEM // 2)]
    cps = [pltpu.make_async_copy(src, dst, sem.at[n]) for n, (src, dst) in enumerate(pairs)]
    for cp in cps:
        cp.start()
    for cp in cps:
        cp.wait()


def per_device(embeddings, codes, codebooks):
    vmem = pl.BlockSpec(memory_space=pltpu.VMEM)
    hbm = pl.BlockSpec(memory_space=pl.ANY)
    dma = pltpu.SemaphoreType.DMA
    by_chunk = (LEVELS, CHUNKS)
    by_block = (LEVELS, N_ITEM // 2, 2, SHARE, DIM)
    books, final = pl.pallas_call(
        main_kernel,
        out_shape=(pltpu.VMEM(by_block, BF16), pltpu.VMEM(embeddings.shape, BF16)),
        in_specs=[hbm, hbm, hbm],
        out_specs=(vmem, vmem),
        scratch_shapes=[
            pltpu.VMEM(codes.shape, I32),
            pltpu.VMEM(embeddings.shape, BF16),
            pltpu.VMEM((ROWS, LANES), I32),
            pltpu.VMEM((LEVELS, SHARE, DIM), BF16),
            pltpu.VMEM((4, 8, LANES), I32),
            pltpu.VMEM((N_ITEM, 8, LANES), I32),
            pltpu.VMEM((*by_chunk, SLOTS, WIDTH), BF16),
            pltpu.VMEM((*by_chunk, SLOTS, WIDTH), BF16),
            pltpu.VMEM((*by_chunk, SLOTS, WIDTH), BF16),
            pltpu.VMEM((*by_chunk, SLOTS, WIDTH), BF16),
            pltpu.VMEM((*by_chunk, N_ITEM * SHARE, WIDTH), BF16),
            pltpu.VMEM((*by_chunk, N_CENTER * HOP1, WIDTH), BF16),
            pltpu.VMEM((*by_chunk, N_CENTER * HOP1, WIDTH), BF16),
            pltpu.VMEM((LEVELS - 1, CHUNKS, N_CENTER * HOP2, WIDTH), BF16),
            pltpu.VMEM((LEVELS - 1, CHUNKS, N_CENTER * HOP2, WIDTH), BF16),
            pltpu.VMEM((CHUNKS, ITEMS, WIDTH), BF16),
            pltpu.VMEM((ITEMS, ITEMS), BF16),
            pltpu.VMEM((LEVELS, SHARE, SLOTS), BF16),
            pltpu.VMEM((LEVELS, SLOTS, SHARE), BF16),
            pltpu.VMEM((LEVELS, SHARE, LANES), F32),
            pltpu.VMEM((LEVELS, N_CENTER * HOP1, SLOTS), BF16),
            pltpu.VMEM((LEVELS, N_CENTER * HOP2, N_CENTER * HOP1), BF16),
            pltpu.VMEM((LEVELS - 1, SLOTS, N_CENTER * HOP2), BF16),
            dma, dma, dma,
            dma, dma,
            dma(by_chunk), dma(by_chunk),
            dma(by_chunk), dma(by_chunk),
            dma(by_chunk), dma((*by_chunk, 9)), dma(by_chunk),
            dma(by_chunk), dma(by_chunk),
            dma(by_chunk), dma(by_chunk),
            dma((CHUNKS,)), dma((CHUNKS, 9)),
            dma(by_chunk),
        ],
        compiler_params=pltpu.CompilerParams(collective_id=0, has_side_effects=True, vmem_limit_bytes=48 << 20),
    )(codes, embeddings, codebooks)
    books, final = pl.pallas_call(
        copy_kernel,
        out_shape=(jax.ShapeDtypeStruct(by_block, BF16), jax.ShapeDtypeStruct(embeddings.shape, BF16)),
        in_specs=[vmem, vmem],
        out_specs=(hbm, hbm),
        scratch_shapes=[dma((4 + LEVELS * N_ITEM // 2,))],
        compiler_params=pltpu.CompilerParams(vmem_limit_bytes=4 << 20),
    )(books, final)
    return books.reshape(codebooks.shape), final


def solution(mesh):
    placed = (P("item", None), P(None, "item"), P(None, "center", None))
    return jax.shard_map(
        per_device,
        mesh=mesh,
        in_specs=placed,
        out_specs=(P(None, "center", None), P("item", None)),
        check_vma=False,
    )
```

```python
import functools

import jax
import jax.numpy as jnp
from jax import lax
from jax.experimental import pallas as pl
from jax.experimental.pallas import tpu as pltpu
from jax.sharding import PartitionSpec as P

MESH = pl.DeviceIdType.MESH
LEVELS, ITEMS, DIM = 3, 2048, 512
N_ITEM, N_CENTER, SHARE, CAP = 16, 8, 128, 32
SLOTS = N_ITEM * CAP
HOP1, HOP2, HOME = 64, 80, ITEMS // N_CENTER
LANES = 128
F32, BF16, I32 = jnp.float32, jnp.bfloat16, jnp.int32


def iota(shape, axis):
    return lax.broadcasted_iota(I32, shape, axis)


def onehot(match):
    return match.astype(F32).astype(BF16)


def dot(a, b):
    return jnp.dot(a, b, preferred_element_type=F32)


ROW_OFF = 0
ROW_D1 = 12
ROW_D2 = 24
ROW_D3 = 36
ROW_POS = 48
ROWS = 64


ARRIVALS = [(0, 0), (3, 0), (1, 0), (0, 1), (3, 1), (1, 1), (2, 0), (2, 1)]


def ordered(cls, n_cls, lower=None):
    a, b = iota((LANES, 2 * LANES), 0), iota((LANES, 2 * LANES), 1)
    before = onehot((b >= LANES) | (a < b))
    member = onehot(iota((n_cls, ITEMS), 0) == cls)
    seen = jnp.zeros((n_cls, LANES), F32)
    ranks = []
    for k in range(ITEMS // LANES):
        part = member[:, k * LANES : (k + 1) * LANES]
        both = dot(part, before)
        ranks.append(jnp.sum(part.astype(F32) * (both[:, :LANES] + seen), axis=0, keepdims=True))
        seen = seen + both[:, LANES:]
    rank = jnp.concatenate(ranks, axis=1).astype(I32)
    if lower is None:
        return rank, None
    r, s = iota((n_cls, n_cls), 0), iota((n_cls, n_cls), 1)
    start = jnp.dot(lower(r, s).astype(F32), seen, precision=lax.Precision.HIGHEST, preferred_element_type=F32)
    start = jnp.concatenate([start] * (ITEMS // LANES), axis=1)
    return rank, jnp.sum(member.astype(F32) * start, axis=0, keepdims=True).astype(I32)


def extract(pos, n_pos, attrs):
    n_hi = n_pos // LANES
    low = onehot(iota((LANES, ITEMS), 0) == jnp.where(pos >= 0, pos & (LANES - 1), -1))
    high = iota((8, ITEMS), 0) == jnp.where(pos >= 0, pos >> 7, -1)
    rows = jnp.concatenate([jnp.where(high, at, 0) for at in attrs], axis=0).astype(F32).astype(BF16)
    got = lax.dot_general(rows, low, (((1,), (1,)), ((), ())), preferred_element_type=F32).astype(I32)
    return [got[8 * k : 8 * k + n_hi] for k in range(len(attrs))]


def slots_of(codes_ref, lev, me):
    code = codes_ref[lev : lev + 1, :]
    shard = code >> 11
    block = jnp.where(shard == me, (code >> 7) & (N_ITEM - 1), -1)
    rank, _ = ordered(block, N_ITEM)
    return shard, code & (SHARE - 1), jnp.where(shard == me, block * CAP + rank, -1)


def prepare_codes(idx, lev, off, local):
    idx[ROW_OFF + 4 * lev : ROW_OFF + 4 * lev + 4, :] = extract(local, SLOTS, [off + 1])[0]


def prepare_moves(idx, lev, me, here, local, there, slot_next):
    if lev < LEVELS - 1:
        rank, start = ordered(here * N_CENTER + there, N_CENTER * N_CENTER, lambda r, s: (r // N_CENTER == s // N_CENTER) & (s < r))
        order = rank + start
        via, place = order & 7, order >> 3
        second, _ = ordered(via * N_CENTER + there, N_CENTER * N_CENTER)
        target = [there + 1, second]
        base = HOP2
        pos3 = jnp.where(there == me, via * HOP2 + second, -1)
        slot_next = jnp.maximum(slot_next, 0)
        hi3, lo3 = extract(pos3, N_CENTER * HOP2, [(slot_next >> 8) + 1, slot_next & 255])
        idx[ROW_D3 + 6 * lev : ROW_D3 + 6 * lev + 5, :] = (hi3 - 1) * 256 + lo3
    else:
        rank, start = ordered(here, N_CENTER, lambda r, s: s < r)
        order = rank + start
        via, place = order & 7, rank >> 3
        target = [jnp.ones_like(order), order >> 3]
        base = HOME
        z, h = (via - me) & 3, (via >> 2) != me // 4
        arrival = jnp.zeros_like(via)
        for n, (dz, dh) in enumerate(ARRIVALS):
            arrival = jnp.where((z == dz) & (h == (dh == 1)), n, arrival)
        for k in range(ITEMS // LANES):
            idx[ROW_POS + k : ROW_POS + k + 1, :] = (arrival * HOME + (order >> 3))[:, k * LANES : (k + 1) * LANES]
    via_s, place_s = extract(local, SLOTS, [via + 1, place])
    idx[ROW_D1 + 4 * lev : ROW_D1 + 4 * lev + 4, :] = (via_s - 1) * HOP1 + place_s
    pos2 = jnp.where(via == me, here * HOP1 + place, -1)
    hi2, lo2 = extract(pos2, N_CENTER * HOP1, target)
    idx[ROW_D2 + 4 * lev : ROW_D2 + 4 * lev + 4, :] = (hi2 - 1) * base + lo2


CHUNKS = 2
TILE = 64
WIDTH = DIM // CHUNKS
ITEM_OFFSETS = sorted([(y, x, c) for y in range(4) for x in range(2) for c in range(2)][1:], key=lambda o: -(4 * o[1] + min(o[0], 4 - o[0])))
CENTER_OFFSETS = sorted([(h, z) for h in range(2) for z in range(4)][1:], key=lambda o: -(2 * o[0] + min(o[1], 4 - o[1])))


def main_kernel(
    codes_hbm, emb_hbm, cb_ref, books_ref, final_ref,
    codes_ref, emb, idx_ref, cb, meta_s, meta_r, dsend, drecv, rsend, rrecv, book, h1s, h1r, h2s, h2r, frecv, scatter, member, members, total,
    sel1, sel2, sel3,
    codes_sem, emb_sem, cb_sem, meta_ss, meta_rs, d_ss, d_rs, r_ss, r_rs, g_ss, g_rs, p_rs, h1_ss, h1_rs, h2_ss, h2_rs, f_ss, f_rs, out_sem,
):
    item, center = lax.axis_index("item"), lax.axis_index("center")
    my_y, my_x, my_c = item // 4, (item // 2) % 2, item % 2
    my_h, my_z = center // 4, center % 4

    def item_at(y, x, c):
        return ((my_y + y) % 4) * 4 + ((my_x + x) % 2) * 2 + (my_c + c) % 2

    def center_at(h, z):
        return ((my_h + h) % 2) * 4 + (my_z + z) % 4

    def rows(start, size, step):
        return pl.ds(pl.multiple_of(start * step, step), size)

    own_codes = pltpu.make_async_copy(codes_hbm, codes_ref, codes_sem)
    own_codes.start()
    own_emb = pltpu.make_async_copy(emb_hbm, emb, emb_sem)
    own_emb.start()
    barrier = pltpu.get_barrier_semaphore()
    for o in ITEM_OFFSETS:
        pl.semaphore_signal(barrier, inc=1, device_id=(item_at(*o), center), device_id_type=MESH)
    for o in CENTER_OFFSETS:
        pl.semaphore_signal(barrier, inc=1, device_id=(item, center_at(*o)), device_id_type=MESH)

    own_cb = pltpu.make_async_copy(cb_ref.at[:, rows(item, SHARE, SHARE), :], cb, cb_sem)
    own_cb.start()

    def remote(src, dst, ss, rs, to):
        return pltpu.make_async_remote_copy(
            src_ref=src, dst_ref=dst, send_sem=ss, recv_sem=rs, device_id=to, device_id_type=MESH
        )

    def send(src, dst, ss, rs, to):
        cp = remote(src, dst, ss, rs, to)
        cp.start()
        return cp

    def whole(ref, ss, rs):
        return remote(ref, ref, ss, rs, (item, center))

    pending = []

    own_codes.wait()
    known = [slots_of(codes_ref, 0, center)]
    for k in range(ITEMS // LANES):
        idx_ref[ROW_POS + k : ROW_POS + k + 1, :] = known[0][2][:, k * LANES : (k + 1) * LANES]

    @pl.loop(0, SLOTS // TILE)
    def _(t):
        at = pl.multiple_of(t * TILE, TILE)
        for k in range(ITEMS // LANES):
            scatter[pl.ds(at, TILE), k * LANES : (k + 1) * LANES] = onehot(
                iota((TILE, LANES), 0) + at == idx_ref[ROW_POS + k : ROW_POS + k + 1, :]
            )

    own_emb.wait()

    def send_metas():
        for lev in range(1, LEVELS):
            known.append(slots_of(codes_ref, lev, center))
        for lev in range(LEVELS):
            prepare_codes(idx_ref, lev, *known[lev][1:])
        meta_s[...] = jnp.zeros_like(meta_s)
        for h in range(4):
            for lev in range(LEVELS):
                meta_s[h, lev : lev + 1, :] = idx_ref[ROW_OFF + 4 * lev + h : ROW_OFF + 4 * lev + h + 1, :]
        for o in ITEM_OFFSETS:
            to = item_at(*o)
            send(meta_s.at[to // 4], meta_r.at[item], meta_ss, meta_rs, (to, center))
        meta_r[item] = meta_s[item // 4]
        pending.append(whole(meta_r.at[pl.ds(0, 15)], meta_ss, meta_rs))

    def selection(ref, first, n_in, n_out):
        @pl.loop(0, n_out // TILE)
        def _(t):
            at = pl.multiple_of(t * TILE, TILE)
            for k in range(n_in // LANES):
                ref[pl.ds(at, TILE), k * LANES : (k + 1) * LANES] = onehot(
                    iota((TILE, LANES), 0) + at == idx_ref[first + k : first + k + 1, :]
                )

    def select(ref, n_in, n_out, source):
        return dot(ref[0:n_out, 0:n_in], source).astype(BF16)

    def receive_metas():
        whole(meta_r.at[pl.ds(0, 15)], meta_ss, meta_rs).wait_recv()
        own_cb.wait()
        lane = iota((8, LANES), 1)
        mine = (lane >= (item % 4) * CAP) & (lane < (item % 4 + 1) * CAP)
        for q in range(4):
            codes = jnp.zeros((8, LANES), I32)
            for j in range(4):
                piece = jnp.where(mine, meta_r[4 * q + j], 0)
                codes = codes + pltpu.roll(piece, ((j + 4 - item % 4) % 4) * CAP, 1)
            for lev in range(LEVELS):
                part = (iota((SHARE, LANES), 0) + 1 == codes[lev : lev + 1, :]).astype(F32)
                member[lev, :, q * LANES : (q + 1) * LANES] = part.astype(BF16)
                members[lev, q * LANES : (q + 1) * LANES, :] = part.T.astype(BF16)
        for lev in range(LEVELS):
            count = jnp.sum(member[lev].astype(F32), axis=1, keepdims=True)
            total[lev] = jnp.broadcast_to(count + 1.0, (SHARE, LANES))

    def moves(lev):
        nxt = known[min(lev + 1, LEVELS - 1)]
        prepare_moves(idx_ref, lev, center, known[lev][0], known[lev][2], nxt[0], nxt[2])

    def first_selection(lev):
        selection(sel1.at[lev], ROW_D1 + 4 * lev, SLOTS, N_CENTER * HOP1)

    def second_selection(lev):
        selection(sel2.at[lev], ROW_D2 + 4 * lev, N_CENTER * HOP1, N_CENTER * HOP2 if lev < LEVELS - 1 else HOME)

    def third_selection(lev):
        selection(sel3.at[lev], ROW_D3 + 6 * lev, N_CENTER * HOP2, SLOTS)

    def build_scatter(n):
        @pl.loop(3 * n, min(3 * n + 3, ITEMS // LANES))
        def _(k):
            row = jnp.broadcast_to(idx_ref[pl.ds(ROW_POS + k, 1), :].astype(F32), (LANES, LANES))
            col = row.T.astype(I32)
            at = pl.ds(pl.multiple_of(k * LANES, LANES), LANES)
            for g in range(ITEMS // LANES):
                scatter[at, g * LANES : (g + 1) * LANES] = onehot(iota((LANES, LANES), 1) + g * LANES == col)

    def mover(buf, size, ring, ss, rs):
        def move(n, at, to, part=None):
            index = ring(*at)[0]
            if part is None:
                piece = buf.at[rows(index, size, size)]
            else:
                piece = buf.at[rows(index * 2 + part, size // 2, size // 2)]
            return send(piece, piece, ss, rs.at[n], ring(*to)[1])

        return move

    own, up, down, over = (0, 0), (1, 0), (3, 0), (0, 1)

    def gather_rows(k):
        move = mover(frecv.at[k], HOME, lambda z, h: (center_at(h, z), (item, center_at(h, z))), f_ss.at[k], f_rs.at[k])
        first = [move(0, own, up), move(1, own, down), move(2, own, over)]
        yield
        first[0].wait_recv()
        a = move(3, down, up, 0)
        first[1].wait_recv()
        d = move(4, up, down, 1)
        first[2].wait_recv()
        rest = [move(5, over, up), move(6, over, down)]
        yield
        a.wait_recv()
        rest.append(move(7, (2, 0), over, 0))
        d.wait_recv()
        rest.append(move(8, (2, 0), over, 1))
        yield
        for cp in rest[:2]:
            cp.wait_recv()
        yield
        for cp in rest[2:]:
            cp.wait_recv()

    def gather_books(lev, k):
        bk, cols = book.at[lev, k], slice(k * WIDTH, (k + 1) * WIDTH)
        move = mover(
            bk, SHARE,
            lambda y, x: (my_c * 8 + item_at(y, x, 0) // 2, (item_at(y, x, 0), center)),
            g_ss.at[lev, k], g_rs.at[lev, k],
        )
        first = [move(0, own, up), move(1, own, down), move(2, own, over)]
        yield
        for cp in first:
            cp.wait_recv()
        second = [move(3, down, up, 0), move(4, up, down, 1), move(5, over, up), move(6, over, down)]
        yield
        second[2].wait_recv()
        third = [move(7, (3, 1), up, 0)]
        second[3].wait_recv()
        third.append(move(8, (1, 1), down, 1))
        yield
        for cp in second[:2] + third:
            cp.wait_recv()
        half = bk.at[rows(my_c, 8 * SHARE, 8 * SHARE)]
        passed = send(half, half, g_ss.at[lev, k], p_rs.at[lev, k], (item_at(0, 0, 1), center))
        yield
        passed.wait_recv()
        for c in range(2):
            for q in range(8):
                pltpu.make_async_copy(
                    bk.at[pl.ds((c * 8 + q) * SHARE, SHARE)], books_ref.at[lev, q, c, :, cols], out_sem.at[lev, k]
                ).start()
        pending.append(whole(bk.at[pl.ds(0, 15 * SHARE)], g_ss.at[lev, k], p_rs.at[lev, k]))

    def exchange(src, dst, size, ss, rs):
        own = rows(center, size, size)
        for o in CENTER_OFFSETS:
            to = center_at(*o)
            send(src.at[rows(to, size, size)], dst.at[own], ss, rs, (item, to))
        dst[own, :] = src[own, :]
        cp = whole(dst.at[pl.ds(0, 7 * size)], ss, rs)
        pending.append(cp)
        return cp

    def place(k, cols, first, stop):
        blocks = [frecv[k, rows(center_at(h, z), HOME, HOME), :] for z, h in ARRIVALS[first:stop]]
        source = jnp.concatenate(blocks, axis=0)
        for t in range(ITEMS // 256):
            at = slice(t * 256, (t + 1) * 256)
            found = dot(scatter[at, first * HOME : stop * HOME], source).astype(BF16)
            final_ref[at, cols] = found if first == 0 else final_ref[at, cols] + found

    def swap(src, dst, ss, rs):
        own_rows = rows(item, CAP, CAP)
        for o in ITEM_OFFSETS:
            to = item_at(*o)
            send(src.at[rows(to, CAP, CAP)], dst.at[own_rows], ss, rs, (to, center))
        dst[own_rows, :] = src[own_rows, :]
        cp = whole(dst.at[pl.ds(0, 15 * CAP)], ss, rs)
        pending.append(cp)
        return cp

    def do(f, *args):
        return lambda: f(*args)

    chores = [
        [send_metas, do(moves, 0)],
        [do(first_selection, 0), do(second_selection, 0)],
        [do(third_selection, 0), do(moves, 1)],
        [do(first_selection, 1), do(second_selection, 1)],
        [do(third_selection, 1)],
        [do(moves, 2)],
        [do(first_selection, 2), do(second_selection, 2)],
        [do(build_scatter, 0)],
        [do(build_scatter, 1)],
        [do(build_scatter, 2)],
        [do(build_scatter, 3)],
        [do(build_scatter, 4)],
        [do(build_scatter, 5)],
        [],
    ]

    def program(k):
        cols = slice(k * WIDTH, (k + 1) * WIDTH)
        last = k == CHUNKS - 1
        background = []

        def idle():
            if last:
                for chore in chores.pop(0):
                    chore()

        def step():
            background[:] = [g for g in background if next(g, 0) is None]

        dsend[0, k] = dot(scatter[0:SLOTS, :], emb[:, cols]).astype(BF16)
        if k == 0:
            pl.semaphore_wait(barrier, len(ITEM_OFFSETS) + len(CENTER_OFFSETS))
        for lev in range(LEVELS):
            arrived = swap(dsend.at[lev, k], drecv.at[lev, k], d_ss.at[lev, k], d_rs.at[lev, k])
            step()
            idle()
            yield
            if lev == 0 and k == 0:
                receive_metas()
            arrived.wait_recv()
            pooled = dot(member[lev], drecv[lev, k])
            size = jnp.concatenate([total[lev]] * (WIDTH // LANES), axis=1)
            updated = ((pooled + cb[lev, :, cols].astype(F32)) / size).astype(BF16)
            rsend[lev, k] = (drecv[lev, k].astype(F32) - dot(members[lev], updated)).astype(BF16)
            arrived = swap(rsend.at[lev, k], rrecv.at[lev, k], r_ss.at[lev, k], r_rs.at[lev, k])
            book[lev, k, rows(my_c * 8 + item // 2, SHARE, SHARE), :] = updated
            step()
            fresh = gather_books(lev, k)
            idle()
            yield
            arrived.wait_recv()
            h1s[lev, k] = select(sel1.at[lev], SLOTS, N_CENTER * HOP1, rrecv[lev, k])
            hop = exchange(h1s.at[lev, k], h1r.at[lev, k], HOP1, h1_ss.at[lev, k], h1_rs.at[lev, k])
            step()
            background.append(fresh)
            next(fresh)
            idle()
            yield
            hop.wait_recv()
            if lev < LEVELS - 1:
                h2s[lev, k] = select(sel2.at[lev], N_CENTER * HOP1, N_CENTER * HOP2, h1r[lev, k])
                hop = exchange(h2s.at[lev, k], h2r.at[lev, k], HOP2, h2_ss.at[lev, k], h2_rs.at[lev, k])
                step()
                idle()
                yield
                hop.wait_recv()
                dsend[lev + 1, k] = select(sel3.at[lev], N_CENTER * HOP2, SLOTS, h2r[lev, k])
            else:
                frecv[k, rows(center, HOME, HOME), :] = select(sel2.at[lev], N_CENTER * HOP1, HOME, h1r[lev, k])
                phases = gather_rows(k)
                for phase in range(3):
                    next(phases)
                    step()
                    idle()
                    if phase == 2:
                        place(k, cols, 0, 4)
                    yield
                next(phases)
                place(k, cols, 4, 7)
                next(phases, 0)
                while background:
                    step()
                place(k, cols, 7, 8)
                pending.append(whole(frecv.at[k, pl.ds(0, 7 * HOME)], f_ss.at[k], f_rs.at[k, 0]))

    running = [program(k) for k in range(CHUNKS)]
    while running:
        running = [p for p in running if next(p, 0) is None]

    for lev in range(LEVELS):
        for k in range(CHUNKS):
            pltpu.make_async_copy(book.at[lev, k], book.at[lev, k], out_sem.at[lev, k]).wait()
    for cp in pending:
        cp.wait_send()


def copy_kernel(a_ref, b_ref, oa_ref, ob_ref, sem):
    pairs = [(b_ref.at[pl.ds(h * 512, 512)], ob_ref.at[pl.ds(h * 512, 512)]) for h in range(4)]
    pairs += [(a_ref.at[lev, q], oa_ref.at[lev, q]) for lev in range(LEVELS) for q in range(N_ITEM // 2)]
    cps = [pltpu.make_async_copy(src, dst, sem.at[n]) for n, (src, dst) in enumerate(pairs)]
    for cp in cps:
        cp.start()
    for cp in cps:
        cp.wait()


def per_device(embeddings, codes, codebooks):
    vmem = pl.BlockSpec(memory_space=pltpu.VMEM)
    hbm = pl.BlockSpec(memory_space=pl.ANY)
    dma = pltpu.SemaphoreType.DMA
    by_chunk = (LEVELS, CHUNKS)
    by_block = (LEVELS, N_ITEM // 2, 2, SHARE, DIM)
    books, final = pl.pallas_call(
        main_kernel,
        out_shape=(pltpu.VMEM(by_block, BF16), pltpu.VMEM(embeddings.shape, BF16)),
        in_specs=[hbm, hbm, hbm],
        out_specs=(vmem, vmem),
        scratch_shapes=[
            pltpu.VMEM(codes.shape, I32),
            pltpu.VMEM(embeddings.shape, BF16),
            pltpu.VMEM((ROWS, LANES), I32),
            pltpu.VMEM((LEVELS, SHARE, DIM), BF16),
            pltpu.VMEM((4, 8, LANES), I32),
            pltpu.VMEM((N_ITEM, 8, LANES), I32),
            pltpu.VMEM((*by_chunk, SLOTS, WIDTH), BF16),
            pltpu.VMEM((*by_chunk, SLOTS, WIDTH), BF16),
            pltpu.VMEM((*by_chunk, SLOTS, WIDTH), BF16),
            pltpu.VMEM((*by_chunk, SLOTS, WIDTH), BF16),
            pltpu.VMEM((*by_chunk, N_ITEM * SHARE, WIDTH), BF16),
            pltpu.VMEM((*by_chunk, N_CENTER * HOP1, WIDTH), BF16),
            pltpu.VMEM((*by_chunk, N_CENTER * HOP1, WIDTH), BF16),
            pltpu.VMEM((LEVELS - 1, CHUNKS, N_CENTER * HOP2, WIDTH), BF16),
            pltpu.VMEM((LEVELS - 1, CHUNKS, N_CENTER * HOP2, WIDTH), BF16),
            pltpu.VMEM((CHUNKS, ITEMS, WIDTH), BF16),
            pltpu.VMEM((ITEMS, ITEMS), BF16),
            pltpu.VMEM((LEVELS, SHARE, SLOTS), BF16),
            pltpu.VMEM((LEVELS, SLOTS, SHARE), BF16),
            pltpu.VMEM((LEVELS, SHARE, LANES), F32),
            pltpu.VMEM((LEVELS, N_CENTER * HOP1, SLOTS), BF16),
            pltpu.VMEM((LEVELS, N_CENTER * HOP2, N_CENTER * HOP1), BF16),
            pltpu.VMEM((LEVELS - 1, SLOTS, N_CENTER * HOP2), BF16),
            dma, dma, dma,
            dma, dma,
            dma(by_chunk), dma(by_chunk),
            dma(by_chunk), dma(by_chunk),
            dma(by_chunk), dma((*by_chunk, 9)), dma(by_chunk),
            dma(by_chunk), dma(by_chunk),
            dma(by_chunk), dma(by_chunk),
            dma((CHUNKS,)), dma((CHUNKS, 9)),
            dma(by_chunk),
        ],
        compiler_params=pltpu.CompilerParams(collective_id=0, has_side_effects=True, vmem_limit_bytes=48 << 20),
    )(codes, embeddings, codebooks)
    books, final = pl.pallas_call(
        copy_kernel,
        out_shape=(jax.ShapeDtypeStruct(by_block, BF16), jax.ShapeDtypeStruct(embeddings.shape, BF16)),
        in_specs=[vmem, vmem],
        out_specs=(hbm, hbm),
        scratch_shapes=[dma((4 + LEVELS * N_ITEM // 2,))],
        compiler_params=pltpu.CompilerParams(vmem_limit_bytes=4 << 20),
    )(books, final)
    return books.reshape(codebooks.shape), final


def solution(mesh):
    placed = (P("item", None), P(None, "item"), P(None, "center", None))
    return jax.shard_map(
        per_device,
        mesh=mesh,
        in_specs=placed,
        out_specs=(P(None, "center", None), P("item", None)),
        check_vma=False,
    )
```

```python
import functools

import jax
import jax.numpy as jnp
from jax import lax
from jax.experimental import pallas as pl
from jax.experimental.pallas import tpu as pltpu
from jax.sharding import PartitionSpec as P

MESH = pl.DeviceIdType.MESH
LEVELS, ITEMS, DIM = 3, 2048, 512
N_ITEM, N_CENTER, SHARE, CAP = 16, 8, 128, 32
SLOTS = N_ITEM * CAP
HOP1, HOP2, HOME = 64, 80, ITEMS // N_CENTER
LANES = 128
F32, BF16, I32 = jnp.float32, jnp.bfloat16, jnp.int32


def iota(shape, axis):
    return lax.broadcasted_iota(I32, shape, axis)


def onehot(match):
    return match.astype(F32).astype(BF16)


def dot(a, b):
    return jnp.dot(a, b, preferred_element_type=F32)


ROW_OFF = 0
ROW_D1 = 12
ROW_D2 = 24
ROW_D3 = 36
ROW_POS = 48
ROWS = 64


ARRIVALS = [(0, 0), (3, 0), (1, 0), (0, 1), (3, 1), (1, 1), (2, 0), (2, 1)]


def ordered(cls, n_cls, lower=None):
    a, b = iota((LANES, 2 * LANES), 0), iota((LANES, 2 * LANES), 1)
    before = onehot((b >= LANES) | (a < b))
    member = onehot(iota((n_cls, ITEMS), 0) == cls)
    seen = jnp.zeros((n_cls, LANES), F32)
    ranks = []
    for k in range(ITEMS // LANES):
        part = member[:, k * LANES : (k + 1) * LANES]
        both = dot(part, before)
        ranks.append(jnp.sum(part.astype(F32) * (both[:, :LANES] + seen), axis=0, keepdims=True))
        seen = seen + both[:, LANES:]
    rank = jnp.concatenate(ranks, axis=1).astype(I32)
    if lower is None:
        return rank, None
    r, s = iota((n_cls, n_cls), 0), iota((n_cls, n_cls), 1)
    start = jnp.dot(lower(r, s).astype(F32), seen, precision=lax.Precision.HIGHEST, preferred_element_type=F32)
    start = jnp.concatenate([start] * (ITEMS // LANES), axis=1)
    return rank, jnp.sum(member.astype(F32) * start, axis=0, keepdims=True).astype(I32)


def extract(pos, n_pos, attrs):
    n_hi = n_pos // LANES
    low = onehot(iota((LANES, ITEMS), 0) == jnp.where(pos >= 0, pos & (LANES - 1), -1))
    high = iota((8, ITEMS), 0) == jnp.where(pos >= 0, pos >> 7, -1)
    rows = jnp.concatenate([jnp.where(high, at, 0) for at in attrs], axis=0).astype(F32).astype(BF16)
    got = lax.dot_general(rows, low, (((1,), (1,)), ((), ())), preferred_element_type=F32).astype(I32)
    return [got[8 * k : 8 * k + n_hi] for k in range(len(attrs))]


def slots_of(codes_ref, lev, me):
    code = codes_ref[lev : lev + 1, :]
    shard = code >> 11
    block = jnp.where(shard == me, (code >> 7) & (N_ITEM - 1), -1)
    rank, _ = ordered(block, N_ITEM)
    return shard, code & (SHARE - 1), jnp.where(shard == me, block * CAP + rank, -1)


def prepare_codes(idx, lev, off, local):
    idx[ROW_OFF + 4 * lev : ROW_OFF + 4 * lev + 4, :] = extract(local, SLOTS, [off + 1])[0]


def prepare_moves(idx, lev, me, here, local, there, slot_next):
    if lev < LEVELS - 1:
        rank, start = ordered(here * N_CENTER + there, N_CENTER * N_CENTER, lambda r, s: (r // N_CENTER == s // N_CENTER) & (s < r))
        order = rank + start
        via, place = order & 7, order >> 3
        second, _ = ordered(via * N_CENTER + there, N_CENTER * N_CENTER)
        target = [there + 1, second]
        base = HOP2
        pos3 = jnp.where(there == me, via * HOP2 + second, -1)
        slot_next = jnp.maximum(slot_next, 0)
        hi3, lo3 = extract(pos3, N_CENTER * HOP2, [(slot_next >> 8) + 1, slot_next & 255])
        idx[ROW_D3 + 6 * lev : ROW_D3 + 6 * lev + 5, :] = (hi3 - 1) * 256 + lo3
    else:
        rank, start = ordered(here, N_CENTER, lambda r, s: s < r)
        order = rank + start
        via, place = order & 7, rank >> 3
        target = [jnp.ones_like(order), order >> 3]
        base = HOME
        z, h = (via - me) & 3, (via >> 2) != me // 4
        arrival = jnp.zeros_like(via)
        for n, (dz, dh) in enumerate(ARRIVALS):
            arrival = jnp.where((z == dz) & (h == (dh == 1)), n, arrival)
        for k in range(ITEMS // LANES):
            idx[ROW_POS + k : ROW_POS + k + 1, :] = (arrival * HOME + (order >> 3))[:, k * LANES : (k + 1) * LANES]
    via_s, place_s = extract(local, SLOTS, [via + 1, place])
    idx[ROW_D1 + 4 * lev : ROW_D1 + 4 * lev + 4, :] = (via_s - 1) * HOP1 + place_s
    pos2 = jnp.where(via == me, here * HOP1 + place, -1)
    hi2, lo2 = extract(pos2, N_CENTER * HOP1, target)
    idx[ROW_D2 + 4 * lev : ROW_D2 + 4 * lev + 4, :] = (hi2 - 1) * base + lo2


CHUNKS = 2
TILE = 64
WIDTH = DIM // CHUNKS
ITEM_OFFSETS = sorted([(y, x, c) for y in range(4) for x in range(2) for c in range(2)][1:], key=lambda o: -(4 * o[1] + min(o[0], 4 - o[0])))
CENTER_OFFSETS = sorted([(h, z) for h in range(2) for z in range(4)][1:], key=lambda o: -(2 * o[0] + min(o[1], 4 - o[1])))


def main_kernel(
    codes_hbm, emb_hbm, cb_ref, books_ref, final_ref,
    codes_ref, emb, idx_ref, cb, meta_s, meta_r, dsend, drecv, rsend, rrecv, book, h1s, h1r, h2s, h2r, frecv, scatter, member, members, total,
    sel1, sel2, sel3,
    codes_sem, emb_sem, cb_sem, meta_ss, meta_rs, d_ss, d_rs, r_ss, r_rs, g_ss, g_rs, p_rs, h1_ss, h1_rs, h2_ss, h2_rs, f_ss, f_rs, out_sem,
):
    item, center = lax.axis_index("item"), lax.axis_index("center")
    my_y, my_x, my_c = item // 4, (item // 2) % 2, item % 2
    my_h, my_z = center // 4, center % 4

    def item_at(y, x, c):
        return ((my_y + y) % 4) * 4 + ((my_x + x) % 2) * 2 + (my_c + c) % 2

    def center_at(h, z):
        return ((my_h + h) % 2) * 4 + (my_z + z) % 4

    def rows(start, size, step):
        return pl.ds(pl.multiple_of(start * step, step), size)

    own_codes = pltpu.make_async_copy(codes_hbm, codes_ref, codes_sem)
    own_codes.start()
    own_emb = pltpu.make_async_copy(emb_hbm, emb, emb_sem)
    own_emb.start()
    barrier = pltpu.get_barrier_semaphore()
    for o in ITEM_OFFSETS:
        pl.semaphore_signal(barrier, inc=1, device_id=(item_at(*o), center), device_id_type=MESH)
    for o in CENTER_OFFSETS:
        pl.semaphore_signal(barrier, inc=1, device_id=(item, center_at(*o)), device_id_type=MESH)

    own_cb = pltpu.make_async_copy(cb_ref.at[:, rows(item, SHARE, SHARE), :], cb, cb_sem)
    own_cb.start()

    def remote(src, dst, ss, rs, to):
        return pltpu.make_async_remote_copy(
            src_ref=src, dst_ref=dst, send_sem=ss, recv_sem=rs, device_id=to, device_id_type=MESH
        )

    def send(src, dst, ss, rs, to):
        cp = remote(src, dst, ss, rs, to)
        cp.start()
        return cp

    def whole(ref, ss, rs):
        return remote(ref, ref, ss, rs, (item, center))

    pending = []

    own_codes.wait()
    known = [slots_of(codes_ref, 0, center)]
    for k in range(ITEMS // LANES):
        idx_ref[ROW_POS + k : ROW_POS + k + 1, :] = known[0][2][:, k * LANES : (k + 1) * LANES]

    @pl.loop(0, SLOTS // TILE)
    def _(t):
        at = pl.multiple_of(t * TILE, TILE)
        for k in range(ITEMS // LANES):
            scatter[pl.ds(at, TILE), k * LANES : (k + 1) * LANES] = onehot(
                iota((TILE, LANES), 0) + at == idx_ref[ROW_POS + k : ROW_POS + k + 1, :]
            )

    own_emb.wait()

    def send_metas():
        for lev in range(1, LEVELS):
            known.append(slots_of(codes_ref, lev, center))
        for lev in range(LEVELS):
            prepare_codes(idx_ref, lev, *known[lev][1:])
        meta_s[...] = jnp.zeros_like(meta_s)
        for h in range(4):
            for lev in range(LEVELS):
                meta_s[h, lev : lev + 1, :] = idx_ref[ROW_OFF + 4 * lev + h : ROW_OFF + 4 * lev + h + 1, :]
        for o in ITEM_OFFSETS:
            to = item_at(*o)
            send(meta_s.at[to // 4], meta_r.at[item], meta_ss, meta_rs, (to, center))
        meta_r[item] = meta_s[item // 4]
        pending.append(whole(meta_r.at[pl.ds(0, 15)], meta_ss, meta_rs))

    def selection(ref, first, n_in, n_out):
        @pl.loop(0, n_out // TILE)
        def _(t):
            at = pl.multiple_of(t * TILE, TILE)
            for k in range(n_in // LANES):
                ref[pl.ds(at, TILE), k * LANES : (k + 1) * LANES] = onehot(
                    iota((TILE, LANES), 0) + at == idx_ref[first + k : first + k + 1, :]
                )

    def select(ref, n_in, n_out, source):
        return dot(ref[0:n_out, 0:n_in], source).astype(BF16)

    def receive_metas():
        whole(meta_r.at[pl.ds(0, 15)], meta_ss, meta_rs).wait_recv()
        own_cb.wait()
        lane = iota((8, LANES), 1)
        mine = (lane >= (item % 4) * CAP) & (lane < (item % 4 + 1) * CAP)
        for q in range(4):
            codes = jnp.zeros((8, LANES), I32)
            for j in range(4):
                piece = jnp.where(mine, meta_r[4 * q + j], 0)
                codes = codes + pltpu.roll(piece, ((j + 4 - item % 4) % 4) * CAP, 1)
            for lev in range(LEVELS):
                part = (iota((SHARE, LANES), 0) + 1 == codes[lev : lev + 1, :]).astype(F32)
                member[lev, :, q * LANES : (q + 1) * LANES] = part.astype(BF16)
                members[lev, q * LANES : (q + 1) * LANES, :] = part.T.astype(BF16)
        for lev in range(LEVELS):
            count = jnp.sum(member[lev].astype(F32), axis=1, keepdims=True)
            total[lev] = jnp.broadcast_to(count + 1.0, (SHARE, LANES))

    def moves(lev):
        nxt = known[min(lev + 1, LEVELS - 1)]
        prepare_moves(idx_ref, lev, center, known[lev][0], known[lev][2], nxt[0], nxt[2])

    def first_selection(lev):
        selection(sel1.at[lev], ROW_D1 + 4 * lev, SLOTS, N_CENTER * HOP1)

    def second_selection(lev):
        selection(sel2.at[lev], ROW_D2 + 4 * lev, N_CENTER * HOP1, N_CENTER * HOP2 if lev < LEVELS - 1 else HOME)

    def third_selection(lev):
        selection(sel3.at[lev], ROW_D3 + 6 * lev, N_CENTER * HOP2, SLOTS)

    def build_scatter(n):
        @pl.loop(3 * n, min(3 * n + 3, ITEMS // LANES))
        def _(k):
            row = jnp.broadcast_to(idx_ref[pl.ds(ROW_POS + k, 1), :].astype(F32), (LANES, LANES))
            col = row.T.astype(I32)
            at = pl.ds(pl.multiple_of(k * LANES, LANES), LANES)
            for g in range(ITEMS // LANES):
                scatter[at, g * LANES : (g + 1) * LANES] = onehot(iota((LANES, LANES), 1) + g * LANES == col)

    def mover(buf, size, ring, ss, rs):
        def move(n, at, to, part=None):
            index = ring(*at)[0]
            if part is None:
                piece = buf.at[rows(index, size, size)]
            else:
                piece = buf.at[rows(index * 2 + part, size // 2, size // 2)]
            return send(piece, piece, ss, rs.at[n], ring(*to)[1])

        return move

    own, up, down, over = (0, 0), (1, 0), (3, 0), (0, 1)

    def gather_rows(k):
        move = mover(frecv.at[k], HOME, lambda z, h: (center_at(h, z), (item, center_at(h, z))), f_ss.at[k], f_rs.at[k])
        first = [move(0, own, up), move(1, own, down), move(2, own, over)]
        yield
        first[0].wait_recv()
        a = move(3, down, up, 0)
        first[1].wait_recv()
        d = move(4, up, down, 1)
        first[2].wait_recv()
        rest = [move(5, over, up), move(6, over, down)]
        yield
        a.wait_recv()
        rest.append(move(7, (2, 0), over, 0))
        d.wait_recv()
        rest.append(move(8, (2, 0), over, 1))
        yield
        for cp in rest[:2]:
            cp.wait_recv()
        yield
        for cp in rest[2:]:
            cp.wait_recv()

    def gather_books(lev, k):
        bk, cols = book.at[lev, k], slice(k * WIDTH, (k + 1) * WIDTH)
        move = mover(
            bk, SHARE,
            lambda y, x: (my_c * 8 + item_at(y, x, 0) // 2, (item_at(y, x, 0), center)),
            g_ss.at[lev, k], g_rs.at[lev, k],
        )
        first = [move(0, own, up), move(1, own, down), move(2, own, over)]
        yield
        for cp in first:
            cp.wait_recv()
        second = [move(3, down, up, 0), move(4, up, down, 1), move(5, over, up), move(6, over, down)]
        yield
        second[2].wait_recv()
        third = [move(7, (3, 1), up, 0)]
        second[3].wait_recv()
        third.append(move(8, (1, 1), down, 1))
        yield
        for cp in second[:2] + third:
            cp.wait_recv()
        half = bk.at[rows(my_c, 8 * SHARE, 8 * SHARE)]
        passed = send(half, half, g_ss.at[lev, k], p_rs.at[lev, k], (item_at(0, 0, 1), center))
        yield
        passed.wait_recv()
        for c in range(2):
            for q in range(8):
                pltpu.make_async_copy(
                    bk.at[pl.ds((c * 8 + q) * SHARE, SHARE)], books_ref.at[lev, q, c, :, cols], out_sem.at[lev, k]
                ).start()
        pending.append(whole(bk.at[pl.ds(0, 15 * SHARE)], g_ss.at[lev, k], p_rs.at[lev, k]))

    def exchange(src, dst, size, ss, rs):
        own = rows(center, size, size)
        for o in CENTER_OFFSETS:
            to = center_at(*o)
            send(src.at[rows(to, size, size)], dst.at[own], ss, rs, (item, to))
        dst[own, :] = src[own, :]
        cp = whole(dst.at[pl.ds(0, 7 * size)], ss, rs)
        pending.append(cp)
        return cp

    def place(k, cols, first, stop):
        blocks = [frecv[k, rows(center_at(h, z), HOME, HOME), :] for z, h in ARRIVALS[first:stop]]
        source = jnp.concatenate(blocks, axis=0)
        for t in range(ITEMS // 256):
            at = slice(t * 256, (t + 1) * 256)
            found = dot(scatter[at, first * HOME : stop * HOME], source).astype(BF16)
            final_ref[at, cols] = found if first == 0 else final_ref[at, cols] + found

    def swap(src, dst, ss, rs):
        own_rows = rows(item, CAP, CAP)
        for o in ITEM_OFFSETS:
            to = item_at(*o)
            send(src.at[rows(to, CAP, CAP)], dst.at[own_rows], ss, rs, (to, center))
        dst[own_rows, :] = src[own_rows, :]
        cp = whole(dst.at[pl.ds(0, 15 * CAP)], ss, rs)
        pending.append(cp)
        return cp

    def do(f, *args):
        return lambda: f(*args)

    chores = [
        [send_metas, do(moves, 0)],
        [do(first_selection, 0), do(second_selection, 0)],
        [do(third_selection, 0), do(moves, 1)],
        [do(first_selection, 1), do(second_selection, 1)],
        [do(third_selection, 1)],
        [do(moves, 2)],
        [do(first_selection, 2), do(second_selection, 2)],
        [do(build_scatter, 0)],
        [do(build_scatter, 1)],
        [do(build_scatter, 2)],
        [do(build_scatter, 3)],
        [do(build_scatter, 4)],
        [do(build_scatter, 5)],
        [],
    ]

    def program(k):
        cols = slice(k * WIDTH, (k + 1) * WIDTH)
        last = k == CHUNKS - 1
        background = []

        def idle():
            if last:
                for chore in chores.pop(0):
                    chore()

        def step():
            background[:] = [g for g in background if next(g, 0) is None]

        dsend[0, k] = dot(scatter[0:SLOTS, :], emb[:, cols]).astype(BF16)
        if k == 0:
            pl.semaphore_wait(barrier, len(ITEM_OFFSETS) + len(CENTER_OFFSETS))
        for lev in range(LEVELS):
            arrived = swap(dsend.at[lev, k], drecv.at[lev, k], d_ss.at[lev, k], d_rs.at[lev, k])
            step()
            idle()
            yield
            if lev == 0 and k == 0:
                receive_metas()
            arrived.wait_recv()
            pooled = dot(member[lev], drecv[lev, k])
            size = jnp.concatenate([total[lev]] * (WIDTH // LANES), axis=1)
            updated = ((pooled + cb[lev, :, cols].astype(F32)) / size).astype(BF16)
            rsend[lev, k] = (drecv[lev, k].astype(F32) - dot(members[lev], updated)).astype(BF16)
            arrived = swap(rsend.at[lev, k], rrecv.at[lev, k], r_ss.at[lev, k], r_rs.at[lev, k])
            book[lev, k, rows(my_c * 8 + item // 2, SHARE, SHARE), :] = updated
            step()
            fresh = gather_books(lev, k)
            if lev == LEVELS - 1:
                background.append(fresh)
                next(fresh)
            idle()
            yield
            arrived.wait_recv()
            h1s[lev, k] = select(sel1.at[lev], SLOTS, N_CENTER * HOP1, rrecv[lev, k])
            hop = exchange(h1s.at[lev, k], h1r.at[lev, k], HOP1, h1_ss.at[lev, k], h1_rs.at[lev, k])
            step()
            if lev < LEVELS - 1:
                background.append(fresh)
                next(fresh)
            idle()
            yield
            hop.wait_recv()
            if lev < LEVELS - 1:
                h2s[lev, k] = select(sel2.at[lev], N_CENTER * HOP1, N_CENTER * HOP2, h1r[lev, k])
                hop = exchange(h2s.at[lev, k], h2r.at[lev, k], HOP2, h2_ss.at[lev, k], h2_rs.at[lev, k])
                step()
                idle()
                yield
                hop.wait_recv()
                dsend[lev + 1, k] = select(sel3.at[lev], N_CENTER * HOP2, SLOTS, h2r[lev, k])
            else:
                frecv[k, rows(center, HOME, HOME), :] = select(sel2.at[lev], N_CENTER * HOP1, HOME, h1r[lev, k])
                phases = gather_rows(k)
                for phase in range(3):
                    next(phases)
                    step()
                    idle()
                    if phase == 2:
                        place(k, cols, 0, 4)
                    yield
                next(phases)
                place(k, cols, 4, 7)
                next(phases, 0)
                while background:
                    step()
                place(k, cols, 7, 8)
                pending.append(whole(frecv.at[k, pl.ds(0, 7 * HOME)], f_ss.at[k], f_rs.at[k, 0]))

    running = [program(k) for k in range(CHUNKS)]
    while running:
        running = [p for p in running if next(p, 0) is None]

    for lev in range(LEVELS):
        for k in range(CHUNKS):
            pltpu.make_async_copy(book.at[lev, k], book.at[lev, k], out_sem.at[lev, k]).wait()
    for cp in pending:
        cp.wait_send()


def copy_kernel(a_ref, b_ref, oa_ref, ob_ref, sem):
    pairs = [(b_ref.at[pl.ds(h * 512, 512)], ob_ref.at[pl.ds(h * 512, 512)]) for h in range(4)]
    pairs += [(a_ref.at[lev, q], oa_ref.at[lev, q]) for lev in range(LEVELS) for q in range(N_ITEM // 2)]
    cps = [pltpu.make_async_copy(src, dst, sem.at[n]) for n, (src, dst) in enumerate(pairs)]
    for cp in cps:
        cp.start()
    for cp in cps:
        cp.wait()


def per_device(embeddings, codes, codebooks):
    vmem = pl.BlockSpec(memory_space=pltpu.VMEM)
    hbm = pl.BlockSpec(memory_space=pl.ANY)
    dma = pltpu.SemaphoreType.DMA
    by_chunk = (LEVELS, CHUNKS)
    by_block = (LEVELS, N_ITEM // 2, 2, SHARE, DIM)
    books, final = pl.pallas_call(
        main_kernel,
        out_shape=(pltpu.VMEM(by_block, BF16), pltpu.VMEM(embeddings.shape, BF16)),
        in_specs=[hbm, hbm, hbm],
        out_specs=(vmem, vmem),
        scratch_shapes=[
            pltpu.VMEM(codes.shape, I32),
            pltpu.VMEM(embeddings.shape, BF16),
            pltpu.VMEM((ROWS, LANES), I32),
            pltpu.VMEM((LEVELS, SHARE, DIM), BF16),
            pltpu.VMEM((4, 8, LANES), I32),
            pltpu.VMEM((N_ITEM, 8, LANES), I32),
            pltpu.VMEM((*by_chunk, SLOTS, WIDTH), BF16),
            pltpu.VMEM((*by_chunk, SLOTS, WIDTH), BF16),
            pltpu.VMEM((*by_chunk, SLOTS, WIDTH), BF16),
            pltpu.VMEM((*by_chunk, SLOTS, WIDTH), BF16),
            pltpu.VMEM((*by_chunk, N_ITEM * SHARE, WIDTH), BF16),
            pltpu.VMEM((*by_chunk, N_CENTER * HOP1, WIDTH), BF16),
            pltpu.VMEM((*by_chunk, N_CENTER * HOP1, WIDTH), BF16),
            pltpu.VMEM((LEVELS - 1, CHUNKS, N_CENTER * HOP2, WIDTH), BF16),
            pltpu.VMEM((LEVELS - 1, CHUNKS, N_CENTER * HOP2, WIDTH), BF16),
            pltpu.VMEM((CHUNKS, ITEMS, WIDTH), BF16),
            pltpu.VMEM((ITEMS, ITEMS), BF16),
            pltpu.VMEM((LEVELS, SHARE, SLOTS), BF16),
            pltpu.VMEM((LEVELS, SLOTS, SHARE), BF16),
            pltpu.VMEM((LEVELS, SHARE, LANES), F32),
            pltpu.VMEM((LEVELS, N_CENTER * HOP1, SLOTS), BF16),
            pltpu.VMEM((LEVELS, N_CENTER * HOP2, N_CENTER * HOP1), BF16),
            pltpu.VMEM((LEVELS - 1, SLOTS, N_CENTER * HOP2), BF16),
            dma, dma, dma,
            dma, dma,
            dma(by_chunk), dma(by_chunk),
            dma(by_chunk), dma(by_chunk),
            dma(by_chunk), dma((*by_chunk, 9)), dma(by_chunk),
            dma(by_chunk), dma(by_chunk),
            dma(by_chunk), dma(by_chunk),
            dma((CHUNKS,)), dma((CHUNKS, 9)),
            dma(by_chunk),
        ],
        compiler_params=pltpu.CompilerParams(collective_id=0, has_side_effects=True, vmem_limit_bytes=48 << 20),
    )(codes, embeddings, codebooks)
    books, final = pl.pallas_call(
        copy_kernel,
        out_shape=(jax.ShapeDtypeStruct(by_block, BF16), jax.ShapeDtypeStruct(embeddings.shape, BF16)),
        in_specs=[vmem, vmem],
        out_specs=(hbm, hbm),
        scratch_shapes=[dma((4 + LEVELS * N_ITEM // 2,))],
        compiler_params=pltpu.CompilerParams(vmem_limit_bytes=4 << 20),
    )(books, final)
    return books.reshape(codebooks.shape), final


def solution(mesh):
    placed = (P("item", None), P(None, "item"), P(None, "center", None))
    return jax.shard_map(
        per_device,
        mesh=mesh,
        in_specs=placed,
        out_specs=(P(None, "center", None), P("item", None)),
        check_vma=False,
    )
```
